256 devices in a mesh: group: 32 (over z_hi, x, core), bulk: 8 (over y, z_lo).
Axes of the slice: x: 4, y: 4, z: 8 (z_hi: 4, z_lo: 2; z = z_hi * 2 + z_lo), core: 2. Of those that a mesh axis runs over, the one named last changes fastest.
Arguments:
- picture_feature_vectors: bfloat16 [32, 8, 384, 1152], P('group', 'bulk'), may hold values from -0.1875 to 0.1875
- caption_feature_vectors: bfloat16 [32, 8, 384, 1152], P('group', 'bulk'), may hold values from -0.1875 to 0.1875
- sharpness_factor: float32 [], replicated, may hold values from 4 to 8
- score_offset: float32 [], replicated, may hold values from -4 to -2
- difficult_decoy_tile_numbers: int32 [32, 8, 8, 2], P('group', 'bulk'), may hold values from -1 to 2, as said below
Outputs:
- image_grad: float32 [32, 8, 384, 1152], P('group', 'bulk')
- text_grad: float32 [32, 8, 384, 1152], P('group', 'bulk')
The draws below stay inside these ranges and needn't reach their ends.
Inputs may be any that keep to these rules, and one draw needn't show every extreme that they name: `difficult_decoy_tile_numbers`: toward each bulk index o, the first slots of a device hold block numbers n (rows n * 128 to n * 128 + 127 of the texts of the device with the same group index and bulk index o) and the remaining slots are -1; all slots toward a device's own bulk index are -1; in group index 0 every device with bulk index other than 0 fills all 2 slots toward bulk index 0.
All inputs are finite; a program needn't handle non-finite values.
Results may differ from the reference program's by a relative error of at most 0.0045.
Values may be sent and summed in bfloat16 or wider, within the bound.
No kernel may reach another device: no remote copies, remote signals or barrier semaphores. Data moves between devices by JAX's collectives and lax.ppermute only.
A program may use at most 128 MiB of HBM per device.

```python
import jax
import jax.numpy as jnp
from jax import lax

D = 1152
ROWS = 384
BLOCK = 128
SHIFTS = 4
CAP = 2
NBLK = 3
GROUPS = 32
BULKS = 8


def draw_difficult_decoy_tile_numbers(key, part):
    key = jax.random.fold_in(key, 7)
    heavy_key, light_key, block_key = jax.random.split(key, 3)
    heavy = jax.random.randint(heavy_key, (GROUPS, BULKS, 1, 1), 0, 4) == 0
    light = jax.random.randint(light_key, (GROUPS, BULKS, BULKS, 1), 0, CAP // 2 + 1)
    counts = jnp.where(heavy, CAP, light)
    group_pos = lax.broadcasted_iota(jnp.int32, (GROUPS, BULKS, BULKS, CAP), 0)
    source_pos = lax.broadcasted_iota(jnp.int32, (GROUPS, BULKS, BULKS, CAP), 1)
    owner_pos = lax.broadcasted_iota(jnp.int32, (GROUPS, BULKS, BULKS, CAP), 2)
    slot_pos = lax.broadcasted_iota(jnp.int32, (GROUPS, BULKS, BULKS, CAP), 3)
    forced = jnp.logical_and(group_pos == 0, owner_pos == 0)
    counts = jnp.where(forced, CAP, counts)
    counts = jnp.where(source_pos == owner_pos, 0, counts)
    block_ids = jax.random.randint(block_key, (GROUPS, BULKS, BULKS, CAP), 0, NBLK)
    block_ids = jnp.where(jnp.logical_and(forced, slot_pos == 0), NBLK - 1, block_ids)
    return jnp.where(slot_pos < counts, block_ids, -1).astype(jnp.int32)


def steps_of(key, extent, cuts, least, top_value):
    def one(dim, parts):
        draws = jax.random.uniform(jax.random.fold_in(jax.random.fold_in(key, 6), dim), (parts,), jnp.float32, least / len(cuts), top_value / len(cuts))
        return jnp.repeat(jnp.exp(draws), extent[dim] // parts).reshape((-1,) + (1,) * (len(extent) - dim - 1))

    loudness = one(*cuts[0])
    for cut in cuts[1:]:
        loudness = loudness * one(*cut)
    return loudness


def centred(own_key, extent, spread, reach, cuts=(), dtype=jnp.bfloat16):
    result = jax.random.normal(own_key, extent, jnp.float32) * spread
    if len(cuts) > 0:
        result = steps_of(own_key, extent, cuts, -0.22, 0.18) * result
    return jnp.clip(result, min=-reach, max=reach).astype(dtype)


def setup_inputs(seed: int = 0) -> dict:
    seeds = jax.random.split(jax.random.key(seed), 6)
    return {
        "picture_feature_vectors": centred(seeds[0], (GROUPS, BULKS, ROWS, D), 0.03, 0.1875, ((0, 32), (1, 8))),
        "caption_feature_vectors": centred(seeds[1], (GROUPS, BULKS, ROWS, D), 0.03, 0.1875, ((0, 32), (1, 8))),
        "sharpness_factor": jnp.clip(jax.random.uniform(seeds[2], (), jnp.float32, 4.0, 8.0), 4.0, 8.0),
        "score_offset": jnp.clip(jax.random.uniform(seeds[3], (), jnp.float32, -4.0, -2.0), -4.0, -2.0),
        "difficult_decoy_tile_numbers": draw_difficult_decoy_tile_numbers(jax.random.fold_in(seeds[5], 71), 0),
    }


def unit_rows(raw_rows):
    values = raw_rows.astype(jnp.float32)
    length = jnp.sqrt(lax.optimization_barrier(jnp.sum(values * values, axis=-1, keepdims=True)) + 1e-06)
    return (values / length, length)

def build_match_coefficients(similarity_table, sharpness_factor, score_offset, target_sign, filled_entry_flags):
    logistic_chance = jax.nn.sigmoid(sharpness_factor * similarity_table + score_offset)
    objective_slope = jnp.where(target_sign, logistic_chance - 1.0, logistic_chance) * filled_entry_flags
    return (sharpness_factor * objective_slope).astype(jnp.bfloat16)

def merge_repeats(block_ids, slot_grads):
    count_slots = block_ids.shape[-1]
    same_ids = block_ids[..., :, None] == block_ids[..., None, :]
    earlier = jnp.arange(count_slots)[:, None] > jnp.arange(count_slots)[None, :]
    first_slot = jnp.logical_not(jnp.any(jnp.logical_and(same_ids, earlier), axis=-1))
    totals = jnp.einsum('...ce,...esd->...csd', same_ids.astype(jnp.float32), slot_grads, precision=lax.Precision.HIGHEST)
    return totals * first_slot.astype(jnp.float32)[..., None, None]

def through_norm(unit_values, length, grads):
    inner = lax.optimization_barrier(jnp.sum(unit_values * grads, axis=-1, keepdims=True))
    return (grads - unit_values * inner) / length

def reference(picture_feature_vectors, caption_feature_vectors, sharpness_factor, score_offset, difficult_decoy_tile_numbers):
    precision_high = lax.Precision.HIGHEST
    image_unit, image_len = unit_rows(picture_feature_vectors)
    text_unit, text_len = unit_rows(caption_feature_vectors)
    image_wide = lax.optimization_barrier(image_unit.astype(jnp.bfloat16)).astype(jnp.float32)
    text_wide = lax.optimization_barrier(text_unit.astype(jnp.bfloat16)).astype(jnp.float32)
    diagonal = jnp.arange(ROWS)[:, None] == jnp.arange(ROWS)[None, :]
    grad_image = jnp.zeros((GROUPS, BULKS, ROWS, D), jnp.float32)
    grad_text = jnp.zeros((GROUPS, BULKS, ROWS, D), jnp.float32)
    for shift_step in range(SHIFTS + 1):
        held_text = jnp.roll(text_wide, shift_step, axis=0)
        similarity_table = jnp.einsum('gbrd,gbsd->gbrs', image_wide, held_text, precision=precision_high)
        target_sign = jnp.logical_and(diagonal, shift_step == 0)
        match_coefficient_table = lax.optimization_barrier(build_match_coefficients(similarity_table, sharpness_factor, score_offset, target_sign, 1.0)).astype(jnp.float32)
        grad_image = grad_image + jnp.einsum('gbrs,gbsd->gbrd', match_coefficient_table, held_text, precision=precision_high)
        contribution = jnp.einsum('gbrs,gbrd->gbsd', match_coefficient_table, image_wide, precision=precision_high)
        grad_text = grad_text + jnp.roll(contribution, -shift_step, axis=0)
    all_blocks = text_wide.reshape(GROUPS, BULKS, NBLK, BLOCK, D)
    group_index = jnp.arange(GROUPS)[:, None, None]
    block_range = jnp.arange(NBLK)
    for owner in range(BULKS):
        block_ids = difficult_decoy_tile_numbers[:, :, owner, :]
        filled_entry_flags = (block_ids >= 0).astype(jnp.float32)
        safe_ids = jnp.maximum(block_ids, 0)
        fetched = all_blocks[group_index, owner, safe_ids]
        similarity_table = jnp.einsum('gbrd,gbcsd->gbcrs', image_wide, fetched, precision=precision_high)
        match_coefficient_table = build_match_coefficients(similarity_table, sharpness_factor, score_offset, False, filled_entry_flags[..., None, None])
        match_coefficient_table = lax.optimization_barrier(match_coefficient_table).astype(jnp.float32)
        grad_image = grad_image + jnp.einsum('gbcrs,gbcsd->gbrd', match_coefficient_table, fetched, precision=precision_high)
        slot_grads = jnp.einsum('gbcrs,gbrd->gbcsd', match_coefficient_table, image_wide, precision=precision_high)
        merged = lax.optimization_barrier(merge_repeats(block_ids, slot_grads).astype(jnp.bfloat16)).astype(jnp.float32)
        one_hot = (block_ids[..., None] == block_range).astype(jnp.float32)
        added = jnp.einsum('gbcn,gbcsd->gnsd', one_hot, merged, precision=precision_high)
        grad_text = grad_text.at[:, owner].add(added.reshape(GROUPS, ROWS, D))
    image_grad = through_norm(image_unit, image_len, grad_image)
    text_grad = through_norm(text_unit, text_len, grad_text)
    return (image_grad, text_grad)
```

```python
import jax
import jax.numpy as jnp
from jax import lax
from jax.sharding import Mesh, PartitionSpec as P

BLOCK = 128
HALF = 192
GROUP = ("zh", "x", "c")
BULK = ("y", "zl")


def ring(x, axis, by):
    size = lax.axis_size(axis)
    return lax.ppermute(x, axis, [(i, (i + by) % size) for i in range(size)])


def along_group(x, by):
    return lax.ppermute(x, GROUP, [(i, (i + by) % 32) for i in range(32)])


def unit_rows(raw_rows):
    values = raw_rows.astype(jnp.float32)
    length = jnp.sqrt(jnp.sum(values * values, axis=-1, keepdims=True) + 1e-06)
    return (values / length, length)


def scores_of(a, b):
    return lax.dot_general(a, b, (((1,), (1,)), ((), ())), preferred_element_type=jnp.float32)


def rows_of(w, b):
    return lax.dot_general(w, b, (((1,), (0,)), ((), ())), preferred_element_type=jnp.float32)


def columns_of(w, a):
    return lax.dot_general(w, a, (((0,), (0,)), ((), ())), preferred_element_type=jnp.float32)


def through_norm(unit_values, length, grads):
    inner = jnp.sum(unit_values * grads, axis=-1, keepdims=True)
    return (grads - unit_values * inner) / length


def local(pictures, captions, sharpness, offset, tile_numbers):
    bf16 = jnp.bfloat16
    core = lax.axis_index("c")
    y = lax.axis_index("y")
    zl = lax.axis_index("zl")
    ids = tile_numbers[0, 0]
    ids_far = ring(ids, "zl", 1)
    text_unit, text_len = unit_rows(captions[0, 0])
    text = text_unit.astype(bf16)
    image_unit, image_len = unit_rows(pictures[0, 0])
    image = image_unit.astype(bf16)

    text_prev = ring(text, "y", 1)
    text_next = ring(text, "y", -1)
    image_far = ring(image, "zl", 1)
    text_a = along_group(text, 2)
    image_a = along_group(image, -2)
    text_opp = jnp.concatenate(
        [ring(text_prev[:HALF], "y", 1), ring(text_next[HALF:], "y", -1)], axis=0
    )
    text_b = along_group(text_a, 2)
    image_b = along_group(image_a, -2)
    text_s1 = ring(jnp.where(core == 0, text, text_a), "c", 1)
    image_s1 = ring(jnp.where(core == 1, image, image_a), "c", 1)
    text_s2 = ring(jnp.where(core == 0, text_a, text_b), "c", 1)
    image_s2 = ring(jnp.where(core == 1, image_a, image_b), "c", 1)

    def weights(scores):
        return (sharpness * jax.nn.sigmoid(sharpness * scores + offset)).astype(bf16)

    blocks = jnp.arange(3)

    def times(which, owner):
        mine = lax.dynamic_index_in_dim(which, owner, 0, keepdims=False)
        count = jnp.sum((mine[:, None] == blocks[None, :]).astype(bf16), axis=0)
        return jnp.repeat(count, BLOCK)[None, :]

    def hard(texts, step):
        owner = lax.rem(y + step, 4) * 2 + zl
        near = weights(scores_of(image, texts)) * times(ids, owner)
        far = weights(scores_of(image_far, texts)) * times(ids_far, owner)
        return near, far

    near, far = hard(text_opp, 2)
    part = columns_of(near, image) + columns_of(far, image_far)
    grad_image = rows_of(near, text_opp)
    grad_far = rows_of(far, text_opp)
    half_up = ring(part[:HALF].astype(bf16), "y", 1)
    half_down = ring(part[HALF:].astype(bf16), "y", -1)

    near, far = hard(text_next, 1)
    part = columns_of(near, image) + columns_of(far, image_far)
    grad_image = grad_image + rows_of(near, text_next)
    grad_far = grad_far + rows_of(far, text_next)
    up_b = ring(part[HALF:].astype(bf16), "y", 1)
    up_a = ring((part[:HALF] + half_up.astype(jnp.float32)).astype(bf16), "y", 1)

    near, far = hard(text_prev, 3)
    part = columns_of(near, image) + columns_of(far, image_far)
    grad_image = grad_image + rows_of(near, text_prev)
    grad_far = grad_far + rows_of(far, text_prev)
    down_a = ring(part[:HALF].astype(bf16), "y", -1)
    down_b = ring((part[HALF:] + half_down.astype(jnp.float32)).astype(bf16), "y", -1)

    far = weights(scores_of(image_far, text)) * times(ids_far, y * 2 + zl)
    grad_far = grad_far + rows_of(far, text)
    grad_back = ring(grad_far.astype(bf16), "zl", 1)
    grad_text = columns_of(far, image_far)

    scores = scores_of(image, text)
    same = jnp.arange(384)[:, None] == jnp.arange(384)[None, :]
    chance = jax.nn.sigmoid(sharpness * scores + offset)
    w = (sharpness * jnp.where(same, chance - 1.0, chance)).astype(bf16)
    grad_image = grad_image + rows_of(w, text)
    grad_text = grad_text + columns_of(w, image)
    for texts in (text_a, text_s1, text_b, text_s2):
        grad_image = grad_image + rows_of(weights(scores_of(image, texts)), texts)
    for images in (image_a, image_s1, image_b, image_s2):
        grad_text = grad_text + columns_of(weights(scores_of(images, text)), images)

    grad_image = grad_image + grad_back.astype(jnp.float32)
    grad_text = grad_text + jnp.concatenate([up_a, up_b], axis=0).astype(jnp.float32)
    grad_text = grad_text + jnp.concatenate([down_a, down_b], axis=0).astype(jnp.float32)
    image_grad = through_norm(image_unit, image_len, grad_image)
    text_grad = through_norm(text_unit, text_len, grad_text)
    return (image_grad[None, None], text_grad[None, None])


def solution(mesh):
    fine = Mesh(mesh.devices.reshape(4, 4, 2, 4, 2), GROUP + BULK)
    spec = P(GROUP, BULK, None, None)
    return jax.shard_map(
        local,
        mesh=fine,
        in_specs=(spec, spec, P(), P(), spec),
        out_specs=(spec, spec),
        check_vma=False,
    )
```

```python
import functools

import jax
import jax.numpy as jnp
from jax import lax
from jax.experimental import pallas as pl
from jax.experimental.pallas import tpu as pltpu
from jax.sharding import Mesh, PartitionSpec as P

ROWS = 384
HALF = 192
BLOCK = 128
WIDTH = 1152
GROUP = ("zh", "x", "c")
BULK = ("y", "zl")
BF16 = jnp.bfloat16
F32 = jnp.float32
VM = pl.BlockSpec(memory_space=pltpu.VMEM)
SM = pl.BlockSpec(memory_space=pltpu.SMEM)
UNIT = 2 * ROWS * ROWS * WIDTH


def ring(x, axis, by):
    size = lax.axis_size(axis)
    return lax.ppermute(x, axis, [(i, (i + by) % size) for i in range(size)])


def call(body, outs, ins, args, units, scratch=(), name=None, **more):
    cost = pl.CostEstimate(flops=int(units * UNIT), bytes_accessed=8_000_000, transcendentals=0)
    return pl.pallas_call(
        body,
        out_shape=[jax.ShapeDtypeStruct(s, d) for s, d in outs],
        in_specs=ins,
        out_specs=[VM] * len(outs),
        scratch_shapes=list(scratch),
        cost_estimate=cost,
        compiler_params=pltpu.CompilerParams(vmem_limit_bytes=48 * 2**20),
        name=name,
        **more,
    )(*args)


def nt(a, b):
    return lax.dot_general(a, b, (((1,), (1,)), ((), ())), preferred_element_type=F32)


def nn(a, b):
    return lax.dot_general(a, b, (((1,), (0,)), ((), ())), preferred_element_type=F32)


def tn(a, b):
    return lax.dot_general(a, b, (((0,), (0,)), ((), ())), preferred_element_type=F32)


def inverse_length(values):
    return lax.rsqrt(jnp.sum(values * values, axis=-1, keepdims=True) + 1e-06)


def unit_kernel(cap_ref, pic_ref, text_ref, ta_ref, tb_ref, image_ref, wrap_ref):
    x = lax.axis_index("x")
    for k in range(2):
        at = pl.ds(k * HALF, HALF)
        v = cap_ref[at, :].astype(F32)
        t = (v * inverse_length(v)).astype(BF16)
        text_ref[at, :] = t
        (ta_ref, tb_ref)[k][...] = t
        v = pic_ref[at, :].astype(F32)
        i = (v * inverse_length(v)).astype(BF16)
        image_ref[at, :] = i

        @pl.when(x >= 2)
        def _():
            wrap_ref[at, :] = t

        @pl.when(x < 2)
        def _():
            wrap_ref[at, :] = i


def weights(scores, par_ref):
    s = par_ref[0]
    return s * jax.nn.sigmoid(s * scores + par_ref[1])


def slot_count(ids_ref, owner, block):
    hit = [(ids_ref[owner, c] == block).astype(F32) for c in range(2)]
    return hit[0] + hit[1]


def hard_weights(text, x_scr, wt_ref, row, par_ref, ids_ref, far_ref, owner, own):
    for j in range(3):
        at = pl.ds(j * 256, 256)
        scores = nt(text, x_scr[at, :])
        w = weights(scores, par_ref)
        if own and j < 2:
            r = lax.broadcasted_iota(jnp.int32, (ROWS, 256), 0)
            q = lax.broadcasted_iota(jnp.int32, (ROWS, 256), 1) + j * 256
            w = jnp.where(r == q, w - par_ref[0], w)
        w = w.astype(BF16)
        for n in range(3):
            rows = slice(n * BLOCK, (n + 1) * BLOCK)
            far = slot_count(far_ref, owner, n)
            near = 1.0 if own else slot_count(ids_ref, owner, n)
            for h in range(2):
                col = j * 256 + h * 128
                m = near if col < ROWS else far
                part = w[rows, h * 128 : (h + 1) * 128].astype(F32) * m
                wt_ref[pl.ds(row + n * BLOCK, BLOCK), pl.ds(col, 128)] = part.astype(BF16)


def hard_kernel(
    par_ref, ids_ref, far_ref, image_ref, other_ref, text_ref, na_ref, nb_ref, pa_ref, pb_ref,
    gt_ref, next_a_ref, next_b_ref, prev_a_ref, prev_b_ref, wt_ref, x_scr, t_scr,
):
    y, zl = lax.axis_index("y"), lax.axis_index("zl")
    x_scr[:ROWS, :] = image_ref[...]
    x_scr[ROWS:, :] = other_ref[...]
    args = (par_ref, ids_ref, far_ref)
    t_scr[:HALF, :] = na_ref[...]
    t_scr[HALF:, :] = nb_ref[...]
    hard_weights(t_scr[...], x_scr, wt_ref, 0, *args, lax.rem(y + 1, 4) * 2 + zl, False)
    p = nn(wt_ref[pl.ds(0, ROWS), :], x_scr[...])
    next_a_ref[...] = p[:HALF]
    next_b_ref[...] = p[HALF:].astype(BF16)
    t_scr[:HALF, :] = pa_ref[...]
    t_scr[HALF:, :] = pb_ref[...]
    hard_weights(t_scr[...], x_scr, wt_ref, ROWS, *args, lax.rem(y + 3, 4) * 2 + zl, False)
    p = nn(wt_ref[pl.ds(ROWS, ROWS), :], x_scr[...])
    prev_a_ref[...] = p[:HALF].astype(BF16)
    prev_b_ref[...] = p[HALF:]
    hard_weights(text_ref[...], x_scr, wt_ref, 2 * ROWS, *args, y * 2 + zl, True)
    gt_ref[...] = nn(wt_ref[pl.ds(2 * ROWS, ROWS), :], x_scr[...])


def opposite_kernel(
    par_ref, ids_ref, far_ref, image_ref, other_ref, oa_ref, ob_ref,
    ra_ref, rb_ref, wt_ref, x_scr, t_scr,
):
    y, zl = lax.axis_index("y"), lax.axis_index("zl")
    x_scr[:ROWS, :] = image_ref[...]
    x_scr[ROWS:, :] = other_ref[...]
    t_scr[:HALF, :] = oa_ref[...]
    t_scr[HALF:, :] = ob_ref[...]
    owner = lax.rem(y + 2, 4) * 2 + zl
    hard_weights(t_scr[...], x_scr, wt_ref, 0, par_ref, ids_ref, far_ref, owner, False)
    p = nn(wt_ref[...], x_scr[...])
    ra_ref[...] = p[:HALF].astype(BF16)
    rb_ref[...] = p[HALF:].astype(BF16)


def image_kernel(
    wt3_ref, wt_ref, text_ref, na_ref, nb_ref, pa_ref, pb_ref, oa_ref, ob_ref,
    far_ref, near_ref, w_scr, t_scr,
):
    w_scr[: 3 * ROWS, :] = wt3_ref[...]
    w_scr[3 * ROWS :, :] = wt_ref[...]
    for k, ref in enumerate((na_ref, nb_ref, pa_ref, pb_ref)):
        t_scr[k * HALF : (k + 1) * HALF, :] = ref[...]
    t_scr[2 * ROWS : 3 * ROWS, :] = text_ref[...]
    t_scr[6 * HALF : 7 * HALF, :] = oa_ref[...]
    t_scr[7 * HALF :, :] = ob_ref[...]
    far_ref[...] = tn(w_scr[:, ROWS:], t_scr[...]).astype(BF16)
    near_ref[...] = tn(w_scr[:, :ROWS], t_scr[...])


def attend(mine, scr, w_scr, par_ref, count):
    for j in range(count * 3 // 2):
        at = pl.ds(j * 256, 256)
        w_scr[:, at] = weights(nt(mine, scr[at, :]), par_ref).astype(BF16)
    return nn(w_scr[:, : count * ROWS], scr[: count * ROWS, :])


def cycle_kernel(
    par_ref, image_ref, text_ref, ta, t1, tb, t2, ia, i1, ib, i2, gi_ref, gt_ref,
    gi_out, gt_out, scr, w_scr,
):
    for k, ref in enumerate((ta, t1, tb, t2)):
        scr[k * ROWS : (k + 1) * ROWS, :] = ref[...]
    gi_out[...] = gi_ref[...] + attend(image_ref[...], scr, w_scr, par_ref, 4)
    for k, ref in enumerate((ia, i1, ib, i2)):
        scr[k * ROWS : (k + 1) * ROWS, :] = ref[...]
    gt_out[...] = gt_ref[...] + attend(text_ref[...], scr, w_scr, par_ref, 4)


def late_kernel(par_ref, image_ref, text_ref, a, a1, b, b1, out_ref, scr, w_scr, m_scr):
    x = lax.axis_index("x")

    @pl.when(x == 0)
    def _():
        m_scr[...] = image_ref[...]

    @pl.when(x == 3)
    def _():
        m_scr[...] = text_ref[...]

    @pl.when(jnp.logical_or(x == 0, x == 3))
    def _():
        for k, ref in enumerate((a, a1, b, b1)):
            scr[k * ROWS : (k + 1) * ROWS, :] = ref[...]
        out_ref[...] = attend(m_scr[...], scr, w_scr, par_ref, 4)


def add_kernel(na, ra, pb, rb, ua, db):
    ua[...] = (na[...] + ra[...].astype(F32)).astype(BF16)
    db[...] = (pb[...] + rb[...].astype(F32)).astype(BF16)


def through_norm(raw, grads):
    values = raw.astype(F32)
    inv = inverse_length(values)
    unit = values * inv
    inner = jnp.sum(unit * grads, axis=-1, keepdims=True)
    return (grads - unit * inner) * inv


def last_kernel(
    par_ref, pic_ref, cap_ref, image_ref, text_ref, gi_ref, gt_ref, back_ref, late_ref,
    ua, ub, da, db, f, f1, image_out, text_out, scr, w_scr, m_scr, l_scr,
):
    x = lax.axis_index("x")

    @pl.when(x == 1)
    def _():
        m_scr[...] = image_ref[...]

    @pl.when(x == 2)
    def _():
        m_scr[...] = text_ref[...]

    @pl.when(jnp.logical_or(x == 1, x == 2))
    def _():
        scr[:ROWS, :] = f[...]
        scr[ROWS:, :] = f1[...]
        l_scr[...] = attend(m_scr[...], scr, w_scr, par_ref, 2)

    @pl.when(jnp.logical_or(x == 0, x == 3))
    def _():
        l_scr[...] = late_ref[...]

    for k in range(6):
        at = pl.ds(k * 64, 64)
        g = gi_ref[at, :] + back_ref[at, :].astype(F32)
        g = jnp.where(x < 2, g + l_scr[at, :], g)
        image_out[at, :] = through_norm(pic_ref[at, :], g)
        up, down = (ua, da) if k < 3 else (ub, db)
        here = pl.ds((k % 3) * 64, 64)
        g = gt_ref[at, :] + up[here, :].astype(F32) + down[here, :].astype(F32)
        g = jnp.where(x >= 2, g + l_scr[at, :], g)
        text_out[at, :] = through_norm(cap_ref[at, :], g)


def local(pictures, captions, sharpness, offset, tile_numbers):
    pics, caps = pictures[0, 0], captions[0, 0]
    par = jnp.stack([sharpness, offset])
    ids = tile_numbers[0, 0]
    whole, half = ((ROWS, WIDTH), BF16), ((HALF, WIDTH), BF16)
    whole32, half32 = ((ROWS, WIDTH), F32), ((HALF, WIDTH), F32)
    big = pltpu.VMEM((4 * ROWS, WIDTH), BF16)

    ids_far = ring(ids, "zl", 1)
    text, ta, tb, image, wrap = call(
        unit_kernel, [whole, half, half, whole, whole], [VM] * 2, (caps, pics), 1, name="unit"
    )

    prev_a = ring(ta, "y", 1)
    next_b = ring(tb, "y", -1)
    other = ring(image, "zl", 1)
    prev_b = ring(tb, "y", 1)
    next_a = ring(ta, "y", -1)
    text_a = lax.ppermute(text, "x", [(0, 1), (1, 2), (2, 3)])
    image_a = lax.ppermute(image, "x", [(1, 0), (2, 1), (3, 2)])
    turn = lambda x, c: x * 2 + c
    hop = lax.ppermute(
        wrap,
        ("x", "c"),
        [(turn(x, 0), turn(x, 0)) for x in range(4)]
        + [(turn(a, 1), turn(b, 1)) for a, b in ((3, 0), (2, 1), (1, 2), (0, 3))],
    )
    opp_a = ring(prev_a, "y", 1)
    opp_b = ring(next_b, "y", -1)

    def over(pairs):
        sends = []
        for z in range(4):
            for a, b, c, d in pairs:
                sends.append((z * 8 + turn(a, c), (z + d) % 4 * 8 + turn(b, c)))
        return lax.ppermute(hop, GROUP, sends)

    over_a = over([(3, 0, 0, 1), (0, 3, 0, -1), (0, 0, 1, 1), (3, 3, 1, -1)])
    over_b = over([(2, 0, 0, 1), (1, 3, 0, -1), (1, 0, 1, 1), (2, 3, 1, -1)])
    text_b = lax.ppermute(text_a, "x", [(1, 2), (2, 3)])
    image_b = lax.ppermute(image_a, "x", [(1, 0), (2, 1)])
    core = lax.axis_index("c")
    text_1 = ring(jnp.where(core == 0, text, text_a), "c", 1)
    image_1 = ring(jnp.where(core == 1, image, image_a), "c", 1)
    text_2 = ring(jnp.where(core == 0, text_a, text_b), "c", 1)
    image_2 = ring(jnp.where(core == 1, image_a, image_b), "c", 1)

    pair = pltpu.VMEM((2 * ROWS, WIDTH), BF16)
    one = pltpu.VMEM((ROWS, WIDTH), BF16)
    grad_text, next_pa, next_pb, prev_pa, prev_pb, wt3 = call(
        hard_kernel,
        [whole32, half32, half, half, half32, ((3 * ROWS, 2 * ROWS), BF16)],
        [SM] * 3 + [VM] * 7,
        (par, ids, ids_far, image, other, text, next_a, next_b, prev_a, prev_b),
        13,
        [pair, one],
        name="hard",
    )
    up_b = ring(next_pb, "y", 1)
    down_a = ring(prev_pa, "y", -1)
    far_a, far_b, wt = call(
        opposite_kernel,
        [half, half, ((ROWS, 2 * ROWS), BF16)],
        [SM] * 3 + [VM] * 4,
        (par, ids, ids_far, image, other, opp_a, opp_b),
        5,
        [pair, one],
        name="opposite",
    )
    half_up = ring(far_a, "y", 1)
    half_down = ring(far_b, "y", -1)
    grad_far, grad_image = call(
        image_kernel,
        [whole, whole32],
        [VM] * 9,
        (wt3, wt, text, next_a, next_b, prev_a, prev_b, opp_a, opp_b),
        9,
        [pltpu.VMEM((4 * ROWS, 2 * ROWS), BF16), big],
        name="image_side",
    )
    grad_back = ring(grad_far, "zl", 1)

    grad_image, grad_text = call(
        cycle_kernel,
        [whole32, whole32],
        [SM] + [VM] * 12,
        (par, image, text, text_a, text_1, text_b, text_2, image_a, image_1, image_b, image_2,
         grad_image, grad_text),
        17,
        [big, pltpu.VMEM((ROWS, 4 * ROWS), BF16)],
        name="cycle",
    )
    last_a, last_b = call(
        add_kernel, [half, half], [VM] * 4, (next_pa, half_up, prev_pb, half_down), 1, name="add"
    )
    up_a = ring(last_a, "y", 1)
    down_b = ring(last_b, "y", -1)

    over_f = lax.ppermute(over_a, "x", [(0, 1), (3, 2)])
    over_a1 = ring(over_a, "c", 1)
    over_b1 = lax.ppermute(over_b, ("x", "c"), [(turn(0, 1), turn(0, 0)), (turn(3, 0), turn(3, 1))])
    late = call(
        late_kernel,
        [whole32],
        [SM] + [VM] * 6,
        (par, image, text, over_a, over_a1, over_b, over_b1),
        9,
        [big, pltpu.VMEM((ROWS, 4 * ROWS), BF16), one],
        name="late",
    )[0]
    over_f1 = lax.ppermute(over_f, ("x", "c"), [(turn(1, 1), turn(1, 0)), (turn(2, 0), turn(2, 1))])
    image_grad, text_grad = call(
        last_kernel,
        [whole32, whole32],
        [SM] + [VM] * 14,
        (par, pics, caps, image, text, grad_image, grad_text, grad_back, late,
         up_a, up_b, down_a, down_b, over_f, over_f1),
        5,
        [pair, pltpu.VMEM((ROWS, 2 * ROWS), BF16), one, pltpu.VMEM((ROWS, WIDTH), F32)],
        name="last",
    )
    return (image_grad[None, None], text_grad[None, None])


def solution(mesh):
    fine = Mesh(mesh.devices.reshape(4, 4, 2, 4, 2), GROUP + BULK)
    spec = P(GROUP, BULK, None, None)
    return jax.shard_map(
        local,
        mesh=fine,
        in_specs=(spec, spec, P(), P(), spec),
        out_specs=(spec, spec),
        check_vma=False,
    )
```

```python
import jax
import jax.numpy as jnp
from jax import lax
from jax.experimental import pallas as pl
from jax.experimental.pallas import tpu as pltpu
from jax.sharding import Mesh, PartitionSpec as P

ROWS = 384
HALF = 192
BLOCK = 128
WIDTH = 1152
GROUP = ("zh", "x", "c")
BULK = ("y", "zl")
BF16 = jnp.bfloat16
F32 = jnp.float32
VM = pl.BlockSpec(memory_space=pltpu.VMEM)
SM = pl.BlockSpec(memory_space=pltpu.SMEM)
ANY = pl.BlockSpec(memory_space=pl.ANY)
UNIT = 2 * ROWS * ROWS * WIDTH


def ring(x, axis, by):
    size = lax.axis_size(axis)
    return lax.ppermute(x, axis, [(i, (i + by) % size) for i in range(size)])


def call(body, outs, ins, args, units, scratch=(), name=None, **more):
    cost = pl.CostEstimate(flops=int(units * UNIT), bytes_accessed=8_000_000, transcendentals=0)
    return pl.pallas_call(
        body,
        out_shape=[jax.ShapeDtypeStruct(s, d) for s, d in outs],
        in_specs=ins,
        out_specs=[VM] * len(outs),
        scratch_shapes=list(scratch),
        cost_estimate=cost,
        compiler_params=pltpu.CompilerParams(vmem_limit_bytes=48 * 2**20),
        name=name,
        **more,
    )(*args)


def nt(a, b):
    return lax.dot_general(a, b, (((1,), (1,)), ((), ())), preferred_element_type=F32)


def nn(a, b):
    return lax.dot_general(a, b, (((1,), (0,)), ((), ())), preferred_element_type=F32)


def tn(a, b):
    return lax.dot_general(a, b, (((0,), (0,)), ((), ())), preferred_element_type=F32)


def inverse_length(values):
    return lax.rsqrt(jnp.sum(values * values, axis=-1, keepdims=True) + 1e-06)


def unit_kernel(ids_ref, cap_ref, pic_ref, text_ref, image_ref, wrap_ref, turn_ref):
    x, core = lax.axis_index("x"), lax.axis_index("c")
    for k in range(2):
        at = pl.ds(k * HALF, HALF)
        v = cap_ref[at, :].astype(F32)
        t = (v * inverse_length(v)).astype(BF16)
        text_ref[at, :] = t
        v = pic_ref[at, :].astype(F32)
        i = (v * inverse_length(v)).astype(BF16)
        image_ref[at, :] = i
        wrap_ref[at, :] = jnp.where(x >= 2, t, i)
        for j in range(4):
            ahead = jnp.logical_or(x < j, jnp.logical_and(x == j, core == 0))
            turn_ref[j, at, :] = jnp.where(ahead, t, i)
    row = lax.broadcasted_iota(jnp.int32, (16, BLOCK), 0)
    image_ref[pl.ds(ROWS, 16), :] = jnp.zeros((16, WIDTH), BF16)
    for n in range(3):
        count = jnp.zeros((16, BLOCK), F32)
        for owner in range(8):
            hit = [jnp.where(ids_ref[owner, c] == n, 1.0, 0.0) for c in range(2)]
            count = jnp.where(row == owner, hit[0] + hit[1], count)
        image_ref[pl.ds(ROWS, 16), pl.ds(n * BLOCK, BLOCK)] = count.astype(BF16)


def weights(scores, par_ref):
    s = par_ref[0]
    return s * jax.nn.sigmoid(s * scores + par_ref[1])


def slot_count(image_ref, owner, block):
    counts = image_ref[pl.ds(ROWS, 16), pl.ds(block * BLOCK, BLOCK)].astype(F32)
    row = lax.broadcasted_iota(jnp.int32, (16, BLOCK), 0)
    return jnp.sum(jnp.where(row == owner, counts, 0.0), axis=0, keepdims=True)


def hard_weights(text, x_scr, wt_ref, row, par_ref, image_ref, other_ref, owner, own):
    for j in range(3):
        at = pl.ds(j * 256, 256)
        scores = nt(text, x_scr[at, :])
        w = weights(scores, par_ref)
        if own and j < 2:
            r = lax.broadcasted_iota(jnp.int32, (ROWS, 256), 0)
            q = lax.broadcasted_iota(jnp.int32, (ROWS, 256), 1) + j * 256
            w = jnp.where(r == q, w - par_ref[0], w)
        w = w.astype(BF16)
        for n in range(3):
            rows = slice(n * BLOCK, (n + 1) * BLOCK)
            for h in range(2):
                col = j * 256 + h * 128
                part = w[rows, h * 128 : (h + 1) * 128]
                if col >= ROWS or not own:
                    source = image_ref if col < ROWS else other_ref
                    part = (part.astype(F32) * slot_count(source, owner, n)).astype(BF16)
                wt_ref[pl.ds(row + n * BLOCK, BLOCK), pl.ds(col, 128)] = part


def owners():
    y, zl, core = lax.axis_index("y"), lax.axis_index("zl"), lax.axis_index("c")
    return [lax.rem(y + step, 4) * 2 + zl for step in (3 - 2 * core, 1 + 2 * core, 0, 2)]


def hard_kernel(
    par_ref, image_ref, other_ref, text_ref, one_ref, two_ref,
    early_ref, late_ref, gt_ref, wt_ref, x_scr,
):
    x_scr[:ROWS, :] = image_ref[:ROWS, :]
    x_scr[ROWS:, :] = other_ref[:ROWS, :]
    owner = owners()
    for k, ref in enumerate((one_ref, two_ref, text_ref)):
        hard_weights(
            ref[...], x_scr, wt_ref, k * ROWS, par_ref, image_ref, other_ref, owner[k], k == 2
        )
        p = nn(wt_ref[pl.ds(k * ROWS, ROWS), :], x_scr[...])
        if k == 0:
            early_ref[...] = p.astype(BF16)
        else:
            (late_ref, gt_ref)[k - 1][...] = p


def opposite_kernel(
    par_ref, image_ref, other_ref, opp_ref, after_ref, return_ref, wt_ref, x_scr,
):
    x_scr[:ROWS, :] = image_ref[:ROWS, :]
    x_scr[ROWS:, :] = other_ref[:ROWS, :]
    hard_weights(
        opp_ref[...], x_scr, wt_ref, 0, par_ref, image_ref, other_ref, owners()[3], False
    )
    return_ref[...] = nn(wt_ref[...], x_scr[...]).astype(BF16)


def image_kernel(
    wt3_ref, wt_ref, one_ref, two_ref, text_ref, opp_ref, far_ref, near_ref, w_scr, t_scr
):
    w_scr[: 3 * ROWS, :] = wt3_ref[...]
    w_scr[3 * ROWS :, :] = wt_ref[...]
    for k, ref in enumerate((one_ref, two_ref, text_ref, opp_ref)):
        t_scr[k * ROWS : (k + 1) * ROWS, :] = ref[...]
    far_ref[...] = tn(w_scr[:, ROWS:], t_scr[...]).astype(BF16)
    near_ref[...] = tn(w_scr[:, :ROWS], t_scr[...])


def attend(mine, scr, w_scr, par_ref, count):
    for j in range(count * 3 // 2):
        at = pl.ds(j * 256, 256)
        w_scr[:, at] = weights(nt(mine, scr[at, :]), par_ref).astype(BF16)
    return nn(w_scr[:, : count * ROWS], scr[: count * ROWS, :])


def fill(scr, slot, cases):
    for when, read in cases:

        @pl.when(when)
        def _():
            scr[slot * ROWS : (slot + 1) * ROWS, :] = read()


def cycle_kernel(
    par_ref, image_ref, text_ref, own, sib, aw, sa, bw, sb, gi_ref, gt_ref, after_ref,
    gi_out, gt_out, scr, w_scr,
):
    x, core = lax.axis_index("x"), lax.axis_index("c")
    at = lambda ref, i: lambda: ref[jnp.clip(i, 0, 3)]
    whole = lambda ref: lambda: ref[...]
    blank = lambda: jnp.zeros((ROWS, WIDTH), BF16)

    for side in range(2):
        low = side == 0
        d = x if low else 3 - x
        e = core if low else 1 - core
        pos = (lambda v: v) if low else (lambda v: 3 - v)
        fill(scr, 0, [(d >= 1, at(own, pos(d - 1))), (d == 0, whole(aw))])
        fill(scr, 1, [(d >= 2, at(own, pos(d - 2))), (d == 0, whole(bw)), (d == 1, blank)])
        fill(scr, 2, [(d - 1 + e >= 0, at(sib, pos(d - 1 + e))), (d - 1 + e < 0, whole(sa))])
        first = d == 0
        fill(
            scr, 3,
            [(d - 2 + e >= 0, at(sib, pos(d - 2 + e))),
             (jnp.logical_and(first, e == 0), whole(sb)),
             (jnp.logical_and(first, e == 1), whole(sa)),
             (jnp.logical_and(d == 1, e == 0), blank)],
        )
        if low:
            gi_out[...] = gi_ref[...] + attend(image_ref[:ROWS, :], scr, w_scr, par_ref, 4)
        else:
            gt_out[...] = gt_ref[...] + attend(text_ref[...], scr, w_scr, par_ref, 4)


def add_kernel(late_ref, return_ref, after_ref, out_ref):
    out_ref[...] = (late_ref[...] + return_ref[...].astype(F32)).astype(BF16)


def gate_kernel(hop_ref, after_ref, out_ref):
    pass


def through_norm(raw, grads):
    values = raw.astype(F32)
    inv = inverse_length(values)
    unit = values * inv
    inner = jnp.sum(unit * grads, axis=-1, keepdims=True)
    return (grads - unit * inner) * inv


def last_kernel(
    par_ref, pic_ref, cap_ref, image_ref, text_ref, gi_ref, gt_ref, back_ref, early_ref,
    late_ref, f, f1, image_out, text_out, scr, w_scr, m_scr, l_scr,
):
    x = lax.axis_index("x")
    middle = jnp.logical_or(x == 1, x == 2)

    @pl.when(x == 1)
    def _():
        m_scr[...] = image_ref[:ROWS, :]

    @pl.when(x == 2)
    def _():
        m_scr[...] = text_ref[...]

    @pl.when(middle)
    def _():
        scr[:ROWS, :] = f[...]
        scr[ROWS:, :] = f1[...]
        l_scr[...] = attend(m_scr[...], scr, w_scr, par_ref, 2)

    for k in range(6):
        at = pl.ds(k * 64, 64)
        g = gi_ref[at, :] + back_ref[at, :].astype(F32)
        g = jnp.where(x == 1, g + l_scr[at, :], g)
        image_out[at, :] = through_norm(pic_ref[at, :], g)
        g = gt_ref[at, :] + early_ref[at, :].astype(F32) + late_ref[at, :].astype(F32)
        g = jnp.where(x == 2, g + l_scr[at, :], g)
        text_out[at, :] = through_norm(cap_ref[at, :], g)


def local(pictures, captions, sharpness, offset, tile_numbers):
    pics, caps = pictures[0, 0], captions[0, 0]
    par = jnp.stack([sharpness, offset])
    whole, whole32 = ((ROWS, WIDTH), BF16), ((ROWS, WIDTH), F32)
    big = pltpu.VMEM((4 * ROWS, WIDTH), BF16)
    pair = pltpu.VMEM((2 * ROWS, WIDTH), BF16)
    one = pltpu.VMEM((ROWS, WIDTH), BF16)

    text, image, wrap, turns = call(
        unit_kernel,
        [whole, ((ROWS + 16, WIDTH), BF16), whole, ((4, ROWS, WIDTH), BF16)],
        [SM] + [VM] * 2,
        (tile_numbers[0, 0], caps, pics),
        1,
        name="unit",
    )

    def along_y(block, way):
        pairs = []
        for y in range(4):
            pairs += [(y, (y + way) % 4), (4 + y, 4 + (y - way) % 4)]
        return lax.ppermute(block, ("c", "y"), pairs)

    turn = lambda x, c: x * 2 + c
    other = ring(image, "zl", 1)
    text_one = along_y(text, 1)
    text_two = along_y(text, -1)
    hop = lax.ppermute(
        wrap,
        ("x", "c"),
        [(turn(x, 0), turn(x, 0)) for x in range(4)]
        + [(turn(a, 1), turn(b, 1)) for a, b in ((3, 0), (2, 1), (1, 2), (0, 3))],
    )
    own = lax.all_to_all(turns, "x", split_axis=0, concat_axis=0, tiled=True)
    text_opp = along_y(text_one, 1)
    hop = pl.pallas_call(
        gate_kernel,
        out_shape=jax.ShapeDtypeStruct((ROWS, WIDTH), BF16),
        in_specs=[ANY, ANY],
        out_specs=ANY,
        input_output_aliases={0: 0},
        name="gate",
    )(hop, other)

    def over(pairs):
        sends = []
        for z in range(4):
            for a, b, c, d in pairs:
                sends.append((z * 8 + turn(a, c), (z + d) % 4 * 8 + turn(b, c)))
        return lax.ppermute(hop, GROUP, sends)

    over_a = over([(3, 0, 0, 1), (0, 3, 0, -1), (0, 0, 1, 1), (3, 3, 1, -1)])
    over_b = over([(2, 0, 0, 1), (1, 3, 0, -1), (1, 0, 1, 1), (2, 3, 1, -1)])
    sib = ring(own, "c", 1)

    part_early, part_late, grad_text, wt3 = call(
        hard_kernel,
        [whole, whole32, whole32, ((3 * ROWS, 2 * ROWS), BF16)],
        [SM] + [VM] * 5,
        (par, image, other, text, text_one, text_two),
        13,
        [pair],
        name="hard",
    )
    early = along_y(part_early, -1)
    part_opp, wt = call(
        opposite_kernel,
        [whole, ((ROWS, 2 * ROWS), BF16)],
        [SM] + [VM] * 3 + [ANY],
        (par, image, other, text_opp, part_early),
        5,
        [pair],
        name="opposite",
    )
    carried = along_y(part_opp, 1)
    grad_far, grad_image = call(
        image_kernel,
        [whole, whole32],
        [VM] * 6,
        (wt3, wt, text_one, text_two, text, text_opp),
        9,
        [pltpu.VMEM((4 * ROWS, 2 * ROWS), BF16), big],
        name="image_side",
    )
    grad_back = ring(grad_far, "zl", 1)
    part_late = call(
        add_kernel, [whole], [VM, VM, ANY], (part_late, carried, grad_far), 1, name="add"
    )[0]
    late = along_y(part_late, 1)

    over_f = lax.ppermute(over_a, "x", [(0, 1), (3, 2)])
    over_a1 = ring(over_a, "c", 1)
    over_b1 = lax.ppermute(over_b, ("x", "c"), [(turn(0, 1), turn(0, 0)), (turn(3, 0), turn(3, 1))])
    grad_image, grad_text = call(
        cycle_kernel,
        [whole32, whole32],
        [SM] + [VM] * 10 + [ANY],
        (par, image, text, own, sib, over_a, over_a1, over_b, over_b1, grad_image, grad_text,
         part_late),
        17,
        [big, pltpu.VMEM((ROWS, 4 * ROWS), BF16)],
        name="cycle",
    )
    over_f1 = lax.ppermute(over_f, ("x", "c"), [(turn(1, 1), turn(1, 0)), (turn(2, 0), turn(2, 1))])
    image_grad, text_grad = call(
        last_kernel,
        [whole32, whole32],
        [SM] + [VM] * 11,
        (par, pics, caps, image, text, grad_image, grad_text, grad_back, early, late,
         over_f, over_f1),
        5,
        [pair, pltpu.VMEM((ROWS, 2 * ROWS), BF16), one, pltpu.VMEM((ROWS, WIDTH), F32)],
        name="last",
    )
    return (image_grad[None, None], text_grad[None, None])


def solution(mesh):
    fine = Mesh(mesh.devices.reshape(4, 4, 2, 4, 2), GROUP + BULK)
    spec = P(GROUP, BULK, None, None)
    return jax.shard_map(
        local,
        mesh=fine,
        in_specs=(spec, spec, P(), P(), spec),
        out_specs=(spec, spec),
        check_vma=False,
    )
```

```python
import jax
import jax.numpy as jnp
from jax import lax
from jax.experimental import pallas as pl
from jax.experimental.pallas import tpu as pltpu
from jax.sharding import Mesh, PartitionSpec as P

ROWS = 384
HALF = 192
BLOCK = 128
WIDTH = 1152
GROUP = ("zh", "x", "c")
BULK = ("y", "zl")
BF16 = jnp.bfloat16
F32 = jnp.float32
SM = pl.BlockSpec(memory_space=pltpu.SMEM)
ANY = pl.BlockSpec(memory_space=pltpu.HBM)
FREE = pl.BlockSpec(memory_space=pl.ANY)
WHOLE, WHOLE32 = ((ROWS, WIDTH), BF16), ((ROWS, WIDTH), F32)


def vm(rows, width=WIDTH, dtype=BF16):
    return pltpu.VMEM((rows, width), dtype)


def ring(x, axis, by):
    size = lax.axis_size(axis)
    return lax.ppermute(x, axis, [(i, (i + by) % size) for i in range(size)])


def call(body, outs, args, scratch, name, smem=0, space=ANY, limit=60, flops=8_000_000_000):
    def kernel(*refs):
        body(Copies(refs[-1]), *refs[:-1])

    return pl.pallas_call(
        kernel,
        out_shape=[jax.ShapeDtypeStruct(s, d) for s, d in outs],
        in_specs=[SM] * smem + [space] * (len(args) - smem),
        out_specs=[ANY] * len(outs),
        scratch_shapes=list(scratch) + [pltpu.SemaphoreType.DMA((32,))],
        cost_estimate=pl.CostEstimate(flops=flops, bytes_accessed=0, transcendentals=0),
        compiler_params=pltpu.CompilerParams(vmem_limit_bytes=limit * 2**20),
        name=name,
    )(*args)


class Copies:
    def __init__(self, sems):
        self.sems, self.count = sems, 0

    def go(self, src, dst):
        copy = self.of(src, dst)
        copy.start()
        return copy

    def of(self, src, dst):
        copy = pltpu.make_async_copy(src, dst, self.sems.at[self.count])
        self.count += 1
        return copy

    def pick(self, when, src, other, dst):
        copy = self.of(src, dst)
        instead = pltpu.make_async_copy(other, dst, self.sems.at[self.count - 1])
        pl.when(when)(copy.start)
        pl.when(jnp.logical_not(when))(instead.start)
        return copy


def nt(a, b):
    return lax.dot_general(a, b, (((1,), (1,)), ((), ())), preferred_element_type=F32)


def nn(a, b):
    return lax.dot_general(a, b, (((1,), (0,)), ((), ())), preferred_element_type=F32)


def tn(a, b):
    return lax.dot_general(a, b, (((0,), (0,)), ((), ())), preferred_element_type=F32)


def inverse_length(values):
    return lax.rsqrt(jnp.sum(values * values, axis=-1, keepdims=True) + 1e-06)


def unit_kernel(
    copies, ids_ref, cap_ref, pic_ref, text_out, image_out, wrap_out, even_out, low_out,
    cap, pic, text, image, wrap, even, low,
):
    x = lax.axis_index("x")
    come = [
        [copies.go(src.at[pl.ds(k * HALF, HALF)], dst.at[pl.ds(k * HALF, HALF)])
         for src, dst in ((cap_ref, cap), (pic_ref, pic))]
        for k in range(2)
    ]
    row = lax.broadcasted_iota(jnp.int32, (16, BLOCK), 0)
    image[pl.ds(ROWS, 16), :] = jnp.zeros((16, WIDTH), BF16)
    for n in range(3):
        count = jnp.zeros((16, BLOCK), F32)
        for owner in range(8):
            hit = [jnp.where(ids_ref[c, owner] == n, 1.0, 0.0) for c in range(2)]
            count = jnp.where(row == owner, hit[0] + hit[1], count)
        image[pl.ds(ROWS, 16), pl.ds(n * BLOCK, BLOCK)] = count.astype(BF16)
    leave = []
    for k in range(2):
        at = pl.ds(k * HALF, HALF)
        come[k][0].wait()
        v = cap[at, :].astype(F32)
        t = (v * inverse_length(v)).astype(BF16)
        text[at, :] = t
        come[k][1].wait()
        v = pic[at, :].astype(F32)
        i = (v * inverse_length(v)).astype(BF16)
        image[at, :] = i
        wrap[at, :] = jnp.where(x >= 2, t, i)
        even[at, :] = jnp.where(lax.rem(x, 2) == 0, t, i)
        low[at, :] = jnp.where(x < 2, t, i)
        for src, dst in ((text, text_out), (wrap, wrap_out), (even, even_out), (low, low_out)):
            leave.append(copies.go(src.at[at], dst.at[at]))
        if k == 0:
            leave.append(copies.go(image.at[at], image_out.at[at]))
        else:
            rest = pl.ds(HALF, HALF + 16)
            leave.append(copies.go(image.at[rest], image_out.at[rest]))
    for copy in leave:
        copy.wait()


def weights(scores, par_ref):
    half = par_ref[0] * 0.5
    return half + half * jnp.tanh(half * scores + par_ref[1] * 0.5)


def slot_count(counts, owner, block):
    values = counts[pl.ds(0, 16), pl.ds(block * BLOCK, BLOCK)].astype(F32)
    row = lax.broadcasted_iota(jnp.int32, (16, BLOCK), 0)
    return jnp.sum(jnp.where(row == owner, values, 0.0), axis=0, keepdims=True)


def hard_weights(text, x_scr, wt_ref, row, par_ref, near, far, owner, own):
    for j in range(3):
        w = weights(nt(text, x_scr[pl.ds(j * 256, 256), :]), par_ref)
        if own and j < 2:
            r = lax.broadcasted_iota(jnp.int32, (ROWS, 256), 0)
            q = lax.broadcasted_iota(jnp.int32, (ROWS, 256), 1) + j * 256
            w = jnp.where(r == q, w - par_ref[0], w)
        w = w.astype(BF16)
        for n in range(3):
            rows = slice(n * BLOCK, (n + 1) * BLOCK)
            for h in range(2):
                col = j * 256 + h * 128
                part = w[rows, h * 128 : (h + 1) * 128]
                if col >= ROWS or not own:
                    count = slot_count(near if col < ROWS else far, owner, n)
                    part = (part.astype(F32) * count).astype(BF16)
                wt_ref[pl.ds(row + n * BLOCK, BLOCK), pl.ds(col, 128)] = part


def owners():
    y, zl, core = lax.axis_index("y"), lax.axis_index("zl"), lax.axis_index("c")
    return [lax.rem(y + step, 4) * 2 + zl for step in (3 - 2 * core, 1 + 2 * core, 0, 2)]


def fetch_images(copies, image_ref, other_ref, x_scr, near, far):
    rows, rest = pl.ds(0, ROWS), pl.ds(ROWS, 16)
    return [
        copies.go(image_ref.at[rest], near),
        copies.go(other_ref.at[rest], far),
        copies.go(image_ref.at[rows], x_scr.at[rows]),
        copies.go(other_ref.at[rows], x_scr.at[pl.ds(ROWS, ROWS)]),
    ]


def hard_kernel(
    copies, par_ref, image_ref, other_ref, one_ref, two_ref, text_ref, after_ref,
    early_out, late_out, gt_out, wt_out, x_scr, near, far, t_scr, early, late, gt, wt,
):
    images = fetch_images(copies, image_ref, other_ref, x_scr, near, far)
    texts = [copies.go(ref, t_scr.at[k]) for k, ref in enumerate((one_ref, two_ref, text_ref))]
    owner = owners()
    for copy in images:
        copy.wait()
    leave = []
    for k in range(3):
        texts[k].wait()
        hard_weights(t_scr[k], x_scr, wt, k * ROWS, par_ref, near, far, owner[k], k == 2)
        p = nn(wt[pl.ds(k * ROWS, ROWS), :], x_scr[...])
        if k == 0:
            early[...] = p.astype(BF16)
        else:
            (late, gt)[k - 1][...] = p
        src, dst = ((early, early_out), (late, late_out), (gt, gt_out))[k]
        leave.append(copies.go(src, dst))
    leave.append(copies.go(wt, wt_out))
    for copy in leave:
        copy.wait()


def opposite_kernel(
    copies, par_ref, image_ref, other_ref, opp_ref, after_ref, then_ref, return_out, wt_out,
    x_scr, near, far, text, back, wt,
):
    images = fetch_images(copies, image_ref, other_ref, x_scr, near, far)
    images.append(copies.go(opp_ref, text))
    for copy in images:
        copy.wait()
    hard_weights(text[...], x_scr, wt, 0, par_ref, near, far, owners()[3], False)
    leave = [copies.go(wt, wt_out)]
    back[...] = nn(wt[...], x_scr[...]).astype(BF16)
    leave.append(copies.go(back, return_out))
    for copy in leave:
        copy.wait()


def image_kernel(
    copies, wt3_ref, wt_ref, one_ref, two_ref, text_ref, opp_ref, image_ref, from_one,
    from_two, from_three, aw, bw, far_out, near_out, own_out, w_scr, t_scr, far, near,
):
    come = [
        copies.go(wt3_ref, w_scr.at[pl.ds(0, 3 * ROWS)]),
        copies.go(wt_ref, w_scr.at[pl.ds(3 * ROWS, ROWS)]),
    ]
    for k, ref in enumerate((one_ref, two_ref, text_ref, opp_ref)):
        come.append(copies.go(ref, t_scr.at[pl.ds(k * ROWS, ROWS)]))
    image = image_ref.at[pl.ds(0, ROWS)]
    leave = [copies.pick(lax.axis_index("c") == 0, text_ref, image, own_out.at[0])]
    x = lax.axis_index("x")
    inner = jnp.logical_or(x == 1, x == 2)
    for k, ref in enumerate((from_one, from_two)):
        leave.append(copies.go(ref, own_out.at[k + 1]))
    leave.append(copies.pick(inner, from_three, aw, own_out.at[3]))
    leave.append(copies.go(bw, own_out.at[4]))
    for copy in come:
        copy.wait()
    far[...] = tn(w_scr[:, ROWS:], t_scr[...]).astype(BF16)
    leave.append(copies.go(far, far_out))
    near[...] = tn(w_scr[:, :ROWS], t_scr[...])
    leave.append(copies.go(near, near_out))
    for copy in leave:
        copy.wait()


def attend(mine, scr, w_scr, par_ref, count):
    for j in range(count * 3 // 2):
        at = pl.ds(j * 256, 256)
        w_scr[:, at] = weights(nt(mine, scr[at, :]), par_ref).astype(BF16)
    return nn(w_scr[:, : count * ROWS], scr[: count * ROWS, :])


def cycle_kernel(
    copies, par_ref, image_ref, text_ref, own, sib, gi_ref, gt_ref,
    after_ref, early_ref, gi_out, gt_out, image, text, gi, gt, t_scr, i_scr, w_scr,
):
    x, core = lax.axis_index("x"), lax.axis_index("c")
    come = []
    for low, mine_ref, mine, grad_ref, grad, scr in (
        (True, image_ref, image, gi_ref, gi, t_scr),
        (False, text_ref, text, gt_ref, gt, i_scr),
    ):
        d = x if low else 3 - x
        e = core if low else 1 - core
        slot = lambda k: scr.at[pl.ds(k * ROWS, ROWS)]

        def place(i, beyond):
            inside = jnp.bitwise_xor(x, jnp.clip(i if low else 3 - i, 0, 3))
            return jnp.where(i >= 0, inside, beyond)

        swapped = jnp.logical_and(d == 0, e == 1)
        here = [
            copies.go(mine_ref.at[pl.ds(0, ROWS)], mine),
            copies.go(own.at[place(d - 1, 3)], slot(0)),
            copies.go(own.at[place(d - 2, 4)], slot(1)),
            copies.go(sib.at[place(d - 1 + e, 3)], slot(2)),
            copies.go(sib.at[place(d - 2 + e, jnp.where(swapped, 3, 4))], slot(3)),
        ]
        here.append(copies.go(grad_ref, grad))
        come.append(here)
    leave = []
    for here, mine, grad, scr, out in (
        (come[0], image, gi, t_scr, gi_out),
        (come[1], text, gt, i_scr, gt_out),
    ):
        for copy in here:
            copy.wait()
        grad[...] += attend(mine[...], scr, w_scr, par_ref, 4)
        leave.append(copies.go(grad, out))
    for copy in leave:
        copy.wait()


def add_kernel(copies, late_ref, return_ref, after_ref, then_ref, out_ref, late, back, out):
    come = [copies.go(late_ref, late), copies.go(return_ref, back)]
    for copy in come:
        copy.wait()
    out[...] = (late[...] + back[...].astype(F32)).astype(BF16)
    copies.go(out, out_ref).wait()


def gate_kernel(block_ref, after_ref, out_ref):
    pass


def through_norm(raw, grads):
    values = raw.astype(F32)
    inv = inverse_length(values)
    unit = values * inv
    inner = jnp.sum(unit * grads, axis=-1, keepdims=True)
    return (grads - unit * inner) * inv


def last_kernel(
    copies, par_ref, f, f1, image_ref, text_ref, pic_ref, gi_ref, back_ref, cap_ref, gt_ref,
    early_ref, late_ref, image_out, text_out,
    scr, w_scr, mine, more, pic, gi, back, cap, gt, early, late,
):
    x = lax.axis_index("x")
    come = [
        copies.go(f, scr.at[pl.ds(0, ROWS)]),
        copies.go(f1, scr.at[pl.ds(ROWS, ROWS)]),
        copies.pick(x <= 1, image_ref.at[pl.ds(0, ROWS)], text_ref, mine),
    ]
    rest = [
        copies.go(src, dst)
        for src, dst in (
            (pic_ref, pic), (gi_ref, gi), (back_ref, back), (cap_ref, cap), (gt_ref, gt),
            (early_ref, early), (late_ref, late),
        )
    ]
    for copy in come:
        copy.wait()

    @pl.when(jnp.logical_or(x == 1, x == 2))
    def _():
        more[...] = attend(mine[...], scr, w_scr, par_ref, 2)

    for copy in rest:
        copy.wait()
    leave = []
    for k in range(3):
        at = pl.ds(k * BLOCK, BLOCK)
        g = gi[at, :] + back[at, :].astype(F32)
        g = jnp.where(x == 1, g + more[at, :], g)
        gi[at, :] = through_norm(pic[at, :], g)
        leave.append(copies.go(gi.at[at], image_out.at[at]))
        g = gt[at, :] + early[at, :].astype(F32) + late[at, :].astype(F32)
        g = jnp.where(x == 2, g + more[at, :], g)
        gt[at, :] = through_norm(cap[at, :], g)
        leave.append(copies.go(gt.at[at], text_out.at[at]))
    for copy in leave:
        copy.wait()


def gate(block, after):
    return pl.pallas_call(
        gate_kernel,
        out_shape=jax.ShapeDtypeStruct(block.shape, block.dtype),
        in_specs=[FREE, FREE],
        out_specs=FREE,
        input_output_aliases={0: 0},
        compiler_params=pltpu.CompilerParams(vmem_limit_bytes=2**20),
        name="gate",
    )(block, after)


def local(pictures, captions, sharpness, offset, tile_numbers):
    pics, caps = pictures[0, 0], captions[0, 0]
    par = jnp.stack([sharpness, offset])
    counts = [vm(16), vm(16)]
    text, image, wrap, even, low = call(
        unit_kernel,
        [WHOLE, ((ROWS + 16, WIDTH), BF16), WHOLE, WHOLE, WHOLE],
        (tile_numbers[0, 0].T, caps, pics),
        [vm(ROWS), vm(ROWS), vm(ROWS), vm(ROWS + 16), vm(ROWS), vm(ROWS), vm(ROWS)],
        "unit",
        1,
    )

    def along_y(block, way):
        pairs = []
        for y in range(4):
            pairs += [(y, (y + way) % 4), (4 + y, 4 + (y - way) % 4)]
        return lax.ppermute(block, ("c", "y"), pairs)

    turn = lambda x, c: x * 2 + c
    with jax.named_scope("one"):
        text_one = along_y(text, 1)
    with jax.named_scope("other"):
        other = ring(image, "zl", 1)
    with jax.named_scope("two"):
        text_two = along_y(text, -1)
    with jax.named_scope("hop"):
        hop = lax.ppermute(
            wrap,
            ("x", "c"),
            [(turn(x, 0), turn(x, 0)) for x in range(4)]
            + [(turn(a, 1), turn(b, 1)) for a, b in ((3, 0), (2, 1), (1, 2), (0, 3))],
        )
    with jax.named_scope("near"):
        from_one = lax.ppermute(even, "x", [(0, 1), (1, 0), (2, 3), (3, 2)])
    with jax.named_scope("mid"):
        from_three = lax.ppermute(low, "x", [(1, 2), (2, 1)])
    with jax.named_scope("far"):
        from_two = lax.ppermute(gate(low, from_one), "x", [(0, 2), (2, 0), (1, 3), (3, 1)])
    with jax.named_scope("opp"):
        text_opp = along_y(text_one, 1)
    hop = gate(hop, other)

    def over(pairs):
        sends = []
        for z in range(4):
            for a, b, c, d in pairs:
                sends.append((z * 8 + turn(a, c), (z + d) % 4 * 8 + turn(b, c)))
        return lax.ppermute(hop, GROUP, sends)

    with jax.named_scope("over_a"):
        over_a = over([(3, 0, 0, 1), (0, 3, 0, -1), (0, 0, 1, 1), (3, 3, 1, -1)])
    with jax.named_scope("over_b"):
        over_b = over([(2, 0, 0, 1), (1, 3, 0, -1), (1, 0, 1, 1), (2, 3, 1, -1)])

    part_early, part_late, grad_text, wt3 = call(
        hard_kernel,
        [WHOLE, WHOLE32, WHOLE32, ((3 * ROWS, 2 * ROWS), BF16)],
        (par, image, other, text_one, text_two, text, hop),
        [vm(2 * ROWS), *counts, pltpu.VMEM((3, ROWS, WIDTH), BF16), vm(ROWS),
         vm(ROWS, dtype=F32), vm(ROWS, dtype=F32), vm(3 * ROWS, 2 * ROWS)],
        "hard",
        1,
    )
    with jax.named_scope("early"):
        early = along_y(part_early, -1)
    part_opp, wt = call(
        opposite_kernel,
        [WHOLE, ((ROWS, 2 * ROWS), BF16)],
        (par, image, other, text_opp, part_early, from_three),
        [vm(2 * ROWS), *counts, vm(ROWS), vm(ROWS), vm(ROWS, 2 * ROWS)],
        "opposite",
        1,
    )
    with jax.named_scope("carried"):
        carried = along_y(part_opp, 1)
    grad_far, grad_image, own = call(
        image_kernel,
        [WHOLE, WHOLE32, ((5, ROWS, WIDTH), BF16)],
        (wt3, wt, text_one, text_two, text, text_opp, image, from_one, from_two, from_three,
         over_a, over_b),
        [vm(4 * ROWS, 2 * ROWS), vm(4 * ROWS), vm(ROWS), vm(ROWS, dtype=F32)],
        "image_side",
    )
    with jax.named_scope("back"):
        grad_back = ring(grad_far, "zl", 1)
    part_late = call(
        add_kernel,
        [WHOLE],
        (part_late, carried, grad_far, early),
        [vm(ROWS, dtype=F32), vm(ROWS), vm(ROWS)],
        "add",
        flops=1,
    )[0]
    with jax.named_scope("late"):
        late = along_y(part_late, 1)

    with jax.named_scope("sib"):
        sib = ring(gate(own, part_late), "c", 1)

    with jax.named_scope("over_f"):
        over_f = lax.ppermute(over_a, "x", [(0, 1), (3, 2)])
    grad_image, grad_text = call(
        cycle_kernel,
        [WHOLE32, WHOLE32],
        (par, image, text, own, sib, grad_image, grad_text, part_late, early),
        [vm(ROWS), vm(ROWS), vm(ROWS, dtype=F32), vm(ROWS, dtype=F32), vm(4 * ROWS),
         vm(4 * ROWS), vm(ROWS, 4 * ROWS)],
        "cycle",
        1,
        flops=1,
    )
    over_f = gate(over_f, grad_image)
    with jax.named_scope("over_f1"):
        over_f1 = lax.ppermute(
            over_f, ("x", "c"), [(turn(1, 1), turn(1, 0)), (turn(2, 0), turn(2, 1))]
        )
    image_grad, text_grad = call(
        last_kernel,
        [WHOLE32, WHOLE32],
        (par, over_f, over_f1, image, text, pics, grad_image, grad_back, caps, grad_text,
         early, late),
        [vm(2 * ROWS), vm(ROWS, 2 * ROWS), vm(ROWS), vm(ROWS, dtype=F32), vm(ROWS),
         vm(ROWS, dtype=F32), vm(ROWS), vm(ROWS), vm(ROWS, dtype=F32), vm(ROWS), vm(ROWS)],
        "last",
        1,
        FREE,
        24,
    )
    return (image_grad[None, None], text_grad[None, None])


def solution(mesh):
    fine = Mesh(mesh.devices.reshape(4, 4, 2, 4, 2), GROUP + BULK)
    spec = P(GROUP, BULK, None, None)
    return jax.shard_map(
        local,
        mesh=fine,
        in_specs=(spec, spec, P(), P(), spec),
        out_specs=(spec, spec),
        check_vma=False,
    )
```

```python
import jax
import jax.numpy as jnp
from jax import lax
from jax.experimental import pallas as pl
from jax.experimental.pallas import tpu as pltpu
from jax.sharding import Mesh, PartitionSpec as P

ROWS = 384
HALF = 192
BLOCK = 128
WIDTH = 1152
GROUP = ("zh", "x", "c")
BULK = ("y", "zl")
BF16 = jnp.bfloat16
F32 = jnp.float32
SM = pl.BlockSpec(memory_space=pltpu.SMEM)
ANY = pl.BlockSpec(memory_space=pltpu.HBM)
FREE = pl.BlockSpec(memory_space=pl.ANY)
WHOLE, WHOLE32 = ((ROWS, WIDTH), BF16), ((ROWS, WIDTH), F32)


def vm(rows, width=WIDTH, dtype=BF16):
    return pltpu.VMEM((rows, width), dtype)


def ring(x, axis, by):
    size = lax.axis_size(axis)
    return lax.ppermute(x, axis, [(i, (i + by) % size) for i in range(size)])


def call(body, outs, args, scratch, name, smem=0, space=ANY, limit=60, flops=8_000_000_000):
    def kernel(*refs):
        body(Copies(refs[-1]), *refs[:-1])

    return pl.pallas_call(
        kernel,
        out_shape=[jax.ShapeDtypeStruct(s, d) for s, d in outs],
        in_specs=[SM] * smem + [space] * (len(args) - smem),
        out_specs=[ANY] * len(outs),
        scratch_shapes=list(scratch) + [pltpu.SemaphoreType.DMA((40,))],
        cost_estimate=pl.CostEstimate(flops=flops, bytes_accessed=0, transcendentals=0),
        compiler_params=pltpu.CompilerParams(vmem_limit_bytes=limit * 2**20),
        name=name,
    )(*args)


class Copies:
    def __init__(self, sems):
        self.sems, self.count = sems, 0

    def go(self, src, dst):
        copy = self.of(src, dst)
        copy.start()
        return copy

    def of(self, src, dst):
        copy = pltpu.make_async_copy(src, dst, self.sems.at[self.count])
        self.count += 1
        return copy

    def pick(self, when, src, other, dst):
        copy = self.of(src, dst)
        instead = pltpu.make_async_copy(other, dst, self.sems.at[self.count - 1])
        pl.when(when)(copy.start)
        pl.when(jnp.logical_not(when))(instead.start)
        return copy


def nt(a, b):
    return lax.dot_general(a, b, (((1,), (1,)), ((), ())), preferred_element_type=F32)


def nn(a, b):
    return lax.dot_general(a, b, (((1,), (0,)), ((), ())), preferred_element_type=F32)


def tn(a, b):
    return lax.dot_general(a, b, (((0,), (0,)), ((), ())), preferred_element_type=F32)


def inverse_length(values):
    return lax.rsqrt(jnp.sum(values * values, axis=-1, keepdims=True) + 1e-06)


def unit_kernel(
    copies, ids_ref, cap_ref, pic_ref, text_out, image_out, wrap_out, even_out, low_out, mid_out,
    cap, pic, text, image, wrap, even, low,
):
    x = lax.axis_index("x")
    come = [
        [copies.go(src.at[pl.ds(k * HALF, HALF)], dst.at[pl.ds(k * HALF, HALF)])
         for src, dst in ((cap_ref, cap), (pic_ref, pic))]
        for k in range(2)
    ]
    row = lax.broadcasted_iota(jnp.int32, (16, BLOCK), 0)
    image[pl.ds(ROWS, 16), :] = jnp.zeros((16, WIDTH), BF16)
    for n in range(3):
        count = jnp.zeros((16, BLOCK), F32)
        for owner in range(8):
            hit = [jnp.where(ids_ref[c, owner] == n, 1.0, 0.0) for c in range(2)]
            count = jnp.where(row == owner, hit[0] + hit[1], count)
        image[pl.ds(ROWS, 16), pl.ds(n * BLOCK, BLOCK)] = count.astype(BF16)
    leave = []
    for k in range(2):
        at = pl.ds(k * HALF, HALF)
        come[k][0].wait()
        v = cap[at, :].astype(F32)
        t = (v * inverse_length(v)).astype(BF16)
        text[at, :] = t
        come[k][1].wait()
        v = pic[at, :].astype(F32)
        i = (v * inverse_length(v)).astype(BF16)
        image[at, :] = i
        wrap[at, :] = jnp.where(x >= 2, t, i)
        even[at, :] = jnp.where(lax.rem(x, 2) == 0, t, i)
        low[at, :] = jnp.where(x < 2, t, i)
        for src, dst in ((text, text_out), (wrap, wrap_out), (even, even_out), (low, low_out), (low, mid_out)):
            leave.append(copies.go(src.at[at], dst.at[at]))
        if k == 0:
            leave.append(copies.go(image.at[at], image_out.at[at]))
        else:
            rest = pl.ds(HALF, HALF + 16)
            leave.append(copies.go(image.at[rest], image_out.at[rest]))
    for copy in leave:
        copy.wait()


def weights(scores, par_ref):
    half = par_ref[0] * 0.5
    return half + half * jnp.tanh(half * scores + par_ref[1] * 0.5)


def slot_count(counts, owner, block):
    values = counts[pl.ds(0, 16), pl.ds(block * BLOCK, BLOCK)].astype(F32)
    row = lax.broadcasted_iota(jnp.int32, (16, BLOCK), 0)
    return jnp.sum(jnp.where(row == owner, values, 0.0), axis=0, keepdims=True)


def hard_weights(text, x_scr, wt_ref, row, par_ref, near, far, owner, own):
    for j in range(3):
        w = weights(nt(text, x_scr[pl.ds(j * 256, 256), :]), par_ref)
        if own and j < 2:
            r = lax.broadcasted_iota(jnp.int32, (ROWS, 256), 0)
            q = lax.broadcasted_iota(jnp.int32, (ROWS, 256), 1) + j * 256
            w = jnp.where(r == q, w - par_ref[0], w)
        w = w.astype(BF16)
        for n in range(3):
            rows = slice(n * BLOCK, (n + 1) * BLOCK)
            for h in range(2):
                col = j * 256 + h * 128
                part = w[rows, h * 128 : (h + 1) * 128]
                if col >= ROWS or not own:
                    count = slot_count(near if col < ROWS else far, owner, n)
                    part = (part.astype(F32) * count).astype(BF16)
                wt_ref[pl.ds(row + n * BLOCK, BLOCK), pl.ds(col, 128)] = part


def owners():
    y, zl, core = lax.axis_index("y"), lax.axis_index("zl"), lax.axis_index("c")
    return [lax.rem(y + step, 4) * 2 + zl for step in (3 - 2 * core, 1 + 2 * core, 0, 2)]


def fetch_images(copies, image_ref, other_ref, x_scr, near, far):
    rows, rest = pl.ds(0, ROWS), pl.ds(ROWS, 16)
    return [
        copies.go(image_ref.at[rest], near),
        copies.go(other_ref.at[rest], far),
        copies.go(image_ref.at[rows], x_scr.at[rows]),
        copies.go(other_ref.at[rows], x_scr.at[pl.ds(ROWS, ROWS)]),
    ]


def hard_kernel(
    copies, par_ref, image_ref, other_ref, one_ref, two_ref, text_ref, after_ref,
    early_out, late_out, gt_out, wt_out, x_scr, near, far, t_scr, early, late, gt, wt,
):
    images = fetch_images(copies, image_ref, other_ref, x_scr, near, far)
    order = (2, 1, 0)
    refs = (one_ref, two_ref, text_ref)
    texts = [copies.go(refs[order[0]], t_scr.at[order[0]])]
    owner = owners()
    for copy in images:
        copy.wait()
    leave = []
    for n, k in enumerate(order):
        texts[n].wait()
        if n == 0:
            texts += [copies.go(refs[m], t_scr.at[m]) for m in order[1:]]
        at = pl.ds(k * ROWS, ROWS)
        hard_weights(t_scr[k], x_scr, wt, k * ROWS, par_ref, near, far, owner[k], k == 2)
        leave.append(copies.go(wt.at[at], wt_out.at[at]))
        dst, out = ((early, early_out), (late, late_out), (gt, gt_out))[k]
        for h in range(2):
            part = pl.ds(h * HALF, HALF)
            p = nn(wt[pl.ds(k * ROWS + h * HALF, HALF), :], x_scr[...])
            dst[part, :] = p.astype(dst.dtype)
            leave.append(copies.go(dst.at[part], out.at[part]))
    for copy in leave:
        copy.wait()


def opposite_kernel(
    copies, par_ref, image_ref, other_ref, opp_ref, after_ref, then_ref, again_ref, return_out, wt_out,
    x_scr, near, far, text, back, wt,
):
    images = fetch_images(copies, image_ref, other_ref, x_scr, near, far)
    images.append(copies.go(opp_ref, text))
    for copy in images:
        copy.wait()
    hard_weights(text[...], x_scr, wt, 0, par_ref, near, far, owners()[3], False)
    leave = [copies.go(wt, wt_out)]
    for h in range(2):
        part = pl.ds(h * HALF, HALF)
        back[part, :] = nn(wt[part, :], x_scr[...]).astype(BF16)
        leave.append(copies.go(back.at[part], return_out.at[part]))
    for copy in leave:
        copy.wait()


def image_kernel(
    copies, wt3_ref, wt_ref, one_ref, two_ref, text_ref, opp_ref, after_ref, then_ref,
    again_ref, far_out, near_out, w_scr, t_scr, far, near,
):
    come = [copies.go(wt3_ref, w_scr.at[pl.ds(0, 3 * ROWS)])]
    for k, ref in enumerate((one_ref, two_ref, text_ref, opp_ref)):
        come.append(copies.go(ref, t_scr.at[pl.ds(k * ROWS, ROWS)]))
    come.append(copies.go(wt_ref, w_scr.at[pl.ds(3 * ROWS, ROWS)]))
    for copy in come[:3]:
        copy.wait()
    pair = pl.ds(0, 2 * ROWS)
    near[...] = tn(w_scr[pair, :ROWS], t_scr[pair, :])
    for copy in come[3:]:
        copy.wait()
    rest = pl.ds(2 * ROWS, 2 * ROWS)
    near[...] += tn(w_scr[rest, :ROWS], t_scr[rest, :])
    leave = [copies.go(near, near_out)]
    for h in range(2):
        part = pl.ds(h * HALF, HALF)
        far[part, :] = tn(w_scr[:, ROWS:][:, h * HALF : (h + 1) * HALF], t_scr[...]).astype(BF16)
        leave.append(copies.go(far.at[part], far_out.at[part]))
    for copy in leave:
        copy.wait()


def bundle_kernel(
    copies, text_ref, image_ref, from_one, from_two, from_three, aw, bw, after_ref, out_ref, own
):
    x = lax.axis_index("x")
    inner = jnp.logical_or(x == 1, x == 2)
    image = image_ref.at[pl.ds(0, ROWS)]
    come = [
        copies.pick(lax.axis_index("c") == 0, text_ref, image, own.at[0]),
        copies.go(from_one, own.at[1]),
        copies.go(from_two, own.at[2]),
        copies.pick(inner, from_three, aw, own.at[3]),
        copies.go(bw, own.at[4]),
    ]
    leave = []
    for k, copy in enumerate(come):
        copy.wait()
        leave.append(copies.go(own.at[k], out_ref.at[k]))
    for copy in leave:
        copy.wait()


def attend(mine, scr, w_scr, par_ref, first):
    for j in range(3):
        at = pl.ds(first * ROWS + j * 256, 256)
        w_scr[:, at] = weights(nt(mine, scr[at, :]), par_ref).astype(BF16)
    both = pl.ds(first * ROWS, 2 * ROWS)
    return nn(w_scr[:, both], scr[both, :])


def cycle_kernel(
    copies, par_ref, image_ref, text_ref, own, sib, gi_ref, gt_ref,
    after_ref, early_ref, gi_out, gt_out, image, text, gi, gt, t_scr, i_scr, w_scr,
):
    x, core = lax.axis_index("x"), lax.axis_index("c")
    come = []
    for low, mine_ref, mine, scr in (
        (True, image_ref, image, t_scr), (False, text_ref, text, i_scr)
    ):
        d = x if low else 3 - x
        e = core if low else 1 - core
        slot = lambda k: scr.at[pl.ds(k * ROWS, ROWS)]

        def place(i, beyond):
            inside = jnp.bitwise_xor(x, jnp.clip(i if low else 3 - i, 0, 3))
            return jnp.where(i >= 0, inside, beyond)

        swapped = jnp.logical_and(d == 0, e == 1)
        come.append([
            lambda a=mine_ref, b=mine: copies.go(a.at[pl.ds(0, ROWS)], b),
            lambda a=own.at[place(d - 1, 3)], b=slot(0): copies.go(a, b),
            lambda a=own.at[place(d - 2, 4)], b=slot(1): copies.go(a, b),
            lambda a=sib.at[place(d - 1 + e, 3)], b=slot(2): copies.go(a, b),
            lambda a=sib.at[place(d - 2 + e, jnp.where(swapped, 3, 4))], b=slot(3): copies.go(a, b),
        ])
    waiting = [start() for start in come[0][:5]]
    leave = []
    for side, (mine, grad, scr, out) in enumerate(
        ((image, gi, t_scr, gi_out), (text, gt, i_scr, gt_out))
    ):
        for copy in waiting[:3]:
            copy.wait()
        total = copies.go(gi_ref if side == 0 else gt_ref, grad)
        following = [start() for start in come[1][:3]] if side == 0 else []
        p = attend(mine[...], scr, w_scr, par_ref, 0)
        total.wait()
        grad[...] += p
        for copy in waiting[3:]:
            copy.wait()
        if side == 0:
            following += [start() for start in come[1][3:5]]
        for h in range(2):
            part = pl.ds(h * HALF, HALF)
            if h == 0:
                p = attend(mine[...], scr, w_scr, par_ref, 2)
            grad[part, :] += p[h * HALF : (h + 1) * HALF]
            leave.append(copies.go(grad.at[part], out.at[part]))
        waiting = following
    for copy in leave:
        copy.wait()


def add_kernel(copies, late_ref, return_ref, after_ref, then_ref, out_ref, late, back, out):
    parts = [pl.ds(k * BLOCK, BLOCK) for k in range(3)]
    come = [
        (copies.go(late_ref.at[at], late.at[at]), copies.go(return_ref.at[at], back.at[at]))
        for at in parts
    ]
    leave = []
    for at, pair in zip(parts, come):
        for copy in pair:
            copy.wait()
        out[at, :] = (late[at, :] + back[at, :].astype(F32)).astype(BF16)
        leave.append(copies.go(out.at[at], out_ref.at[at]))
    for copy in leave:
        copy.wait()


def gate_kernel(block_ref, after_ref, out_ref):
    pass


def through_norm(raw, grads):
    values = raw.astype(F32)
    inv = inverse_length(values)
    unit = values * inv
    inner = jnp.sum(unit * grads, axis=-1, keepdims=True)
    return (grads - unit * inner) * inv


def last_kernel(
    copies, par_ref, f, f1, image_ref, text_ref, pic_ref, gi_ref, back_ref, cap_ref, gt_ref,
    early_ref, late_ref, image_out, text_out,
    scr, w_scr, mine, more, pic, gi, back, cap, gt, early, late,
):
    x = lax.axis_index("x")
    inner = jnp.logical_or(x == 1, x == 2)
    come = [
        copies.of(f, scr.at[pl.ds(0, ROWS)]),
        copies.of(f1, scr.at[pl.ds(ROWS, ROWS)]),
        copies.of(text_ref, mine),
    ]
    for copy in come[:2]:
        pl.when(inner)(copy.start)
    pl.when(x == 2)(come[2].start)
    first = pltpu.make_async_copy(
        image_ref.at[pl.ds(0, ROWS)], mine, copies.sems.at[copies.count - 1]
    )
    pl.when(x == 1)(first.start)
    parts = [pl.ds(k * BLOCK, BLOCK) for k in range(3)]
    rest = [
        [copies.go(src.at[at], dst.at[at]) for src, dst in (
            (pic_ref, pic), (gi_ref, gi), (back_ref, back), (cap_ref, cap), (gt_ref, gt),
            (early_ref, early), (late_ref, late),
        )]
        for at in parts
    ]

    @pl.when(inner)
    def _():
        for copy in come:
            copy.wait()
        more[...] = attend(mine[...], scr, w_scr, par_ref, 0)

    leave = []
    for at, here in zip(parts, rest):
        for copy in here:
            copy.wait()
        g = gi[at, :] + back[at, :].astype(F32)
        g = jnp.where(x == 1, g + more[at, :], g)
        gi[at, :] = through_norm(pic[at, :], g)
        leave.append(copies.go(gi.at[at], image_out.at[at]))
        g = gt[at, :] + early[at, :].astype(F32) + late[at, :].astype(F32)
        g = jnp.where(x == 2, g + more[at, :], g)
        gt[at, :] = through_norm(cap[at, :], g)
        leave.append(copies.go(gt.at[at], text_out.at[at]))
    for copy in leave:
        copy.wait()


def gate(block, after):
    return pl.pallas_call(
        gate_kernel,
        out_shape=jax.ShapeDtypeStruct(block.shape, block.dtype),
        in_specs=[ANY, ANY],
        out_specs=ANY,
        input_output_aliases={0: 0},
        compiler_params=pltpu.CompilerParams(vmem_limit_bytes=60 * 2**20),
        name="gate",
    )(block, after)


def local(pictures, captions, sharpness, offset, tile_numbers):
    pics, caps = pictures[0, 0], captions[0, 0]
    par = jnp.stack([sharpness, offset])
    counts = [vm(16), vm(16)]
    text, image, wrap, even, low, middle = call(
        unit_kernel,
        [WHOLE, ((ROWS + 16, WIDTH), BF16)] + [WHOLE] * 4,
        (tile_numbers[0, 0].T, caps, pics),
        [vm(ROWS), vm(ROWS), vm(ROWS), vm(ROWS + 16), vm(ROWS), vm(ROWS), vm(ROWS)],
        "unit",
        1,
    )

    def along_y(block, way):
        pairs = []
        for y in range(4):
            pairs += [(y, (y + way) % 4), (4 + y, 4 + (y - way) % 4)]
        return lax.ppermute(block, ("c", "y"), pairs)

    turn = lambda x, c: x * 2 + c
    with jax.named_scope("one"):
        text_one = along_y(text, 1)
    with jax.named_scope("other"):
        other = ring(image, "zl", 1)
    with jax.named_scope("two"):
        text_two = along_y(text, -1)
    with jax.named_scope("near"):
        from_one = lax.ppermute(even, "x", [(0, 1), (1, 0), (2, 3), (3, 2)])
    with jax.named_scope("mid"):
        from_three = lax.ppermute(middle, "x", [(1, 2), (2, 1)])
    with jax.named_scope("far"):
        from_two = lax.ppermute(gate(low, from_one), "x", [(0, 2), (2, 0), (1, 3), (3, 1)])
    with jax.named_scope("opp"):
        text_opp = along_y(text_one, 1)
    wrap = gate(wrap, other)

    def over(pairs):
        sends = []
        for z in range(4):
            for a, b, d in pairs:
                sends += [(z * 8 + turn(a, c), (z + d) % 4 * 8 + turn(b, c)) for c in range(2)]
        return lax.ppermute(wrap, GROUP, sends)

    with jax.named_scope("over_a"):
        over_a = over([(3, 0, 1), (0, 3, -1)])
    with jax.named_scope("over_b"):
        over_b = over([(2, 0, 1), (1, 3, -1)])

    part_early, part_late, grad_text, wt3 = call(
        hard_kernel,
        [WHOLE, WHOLE32, WHOLE32, ((3 * ROWS, 2 * ROWS), BF16)],
        (par, image, other, text_one, text_two, text, from_one),
        [vm(2 * ROWS), *counts, pltpu.VMEM((3, ROWS, WIDTH), BF16), vm(ROWS),
         vm(ROWS, dtype=F32), vm(ROWS, dtype=F32), vm(3 * ROWS, 2 * ROWS)],
        "hard",
        1,
    )
    with jax.named_scope("early"):
        early = along_y(part_early, -1)
    part_opp, wt = call(
        opposite_kernel,
        [WHOLE, ((ROWS, 2 * ROWS), BF16)],
        (par, image, other, text_opp, part_early, from_two, from_three),
        [vm(2 * ROWS), *counts, vm(ROWS), vm(ROWS), vm(ROWS, 2 * ROWS)],
        "opposite",
        1,
    )
    with jax.named_scope("carried"):
        carried = along_y(part_opp, 1)
    grad_far, grad_image = call(
        image_kernel,
        [WHOLE, WHOLE32],
        (wt3, wt, text_one, text_two, text, text_opp, from_one, from_two, from_three),
        [vm(4 * ROWS, 2 * ROWS), vm(4 * ROWS), vm(ROWS), vm(ROWS, dtype=F32)],
        "image_side",
    )
    own = call(
        bundle_kernel,
        [((5, ROWS, WIDTH), BF16)],
        (text, image, from_one, from_two, from_three, over_a, over_b, grad_far),
        [pltpu.VMEM((5, ROWS, WIDTH), BF16)],
        "bundle",
    )[0]
    with jax.named_scope("back"):
        grad_back = ring(grad_far, "zl", 1)
    part_late = call(
        add_kernel,
        [WHOLE],
        (part_late, carried, own, early),
        [vm(ROWS, dtype=F32), vm(ROWS), vm(ROWS)],
        "add",
        flops=1,
    )[0]
    with jax.named_scope("late"):
        late = along_y(part_late, 1)

    with jax.named_scope("sib"):
        sib = ring(own, "c", 1)

    with jax.named_scope("over_f"):
        over_f = lax.ppermute(over_a, "x", [(0, 1), (3, 2)])
    grad_image, grad_text = call(
        cycle_kernel,
        [WHOLE32, WHOLE32],
        (par, image, text, own, sib, grad_image, grad_text, part_late, early),
        [vm(ROWS), vm(ROWS), vm(ROWS, dtype=F32), vm(ROWS, dtype=F32), vm(4 * ROWS),
         vm(4 * ROWS), vm(ROWS, 4 * ROWS)],
        "cycle",
        1,
        flops=1,
    )
    over_f = gate(over_f, grad_image)
    with jax.named_scope("over_f1"):
        over_f1 = lax.ppermute(
            over_f, ("x", "c"), [(turn(1, 1), turn(1, 0)), (turn(2, 0), turn(2, 1))]
        )
    image_grad, text_grad = call(
        last_kernel,
        [WHOLE32, WHOLE32],
        (par, over_f, over_f1, image, text, pics, grad_image, grad_back, caps, grad_text,
         early, late),
        [vm(2 * ROWS), vm(ROWS, 2 * ROWS), vm(ROWS), vm(ROWS, dtype=F32), vm(ROWS),
         vm(ROWS, dtype=F32), vm(ROWS), vm(ROWS), vm(ROWS, dtype=F32), vm(ROWS), vm(ROWS)],
        "last",
        1,
    )
    return (image_grad[None, None], text_grad[None, None])


def solution(mesh):
    fine = Mesh(mesh.devices.reshape(4, 4, 2, 4, 2), GROUP + BULK)
    spec = P(GROUP, BULK, None, None)
    return jax.shard_map(
        local,
        mesh=fine,
        in_specs=(spec, spec, P(), P(), spec),
        out_specs=(spec, spec),
        check_vma=False,
    )
```

```python
import jax
import jax.numpy as jnp
from jax import lax
from jax.experimental import pallas as pl
from jax.experimental.pallas import tpu as pltpu
from jax.sharding import Mesh, PartitionSpec as P

ROWS = 384
HALF = 192
BLOCK = 128
WIDTH = 1152
GROUP = ("zh", "x", "c")
BULK = ("y", "zl")
BF16 = jnp.bfloat16
F32 = jnp.float32
SM = pl.BlockSpec(memory_space=pltpu.SMEM)
ANY = pl.BlockSpec(memory_space=pltpu.HBM)
WHOLE, WHOLE32 = ((ROWS, WIDTH), BF16), ((ROWS, WIDTH), F32)


def vm(rows, width=WIDTH, dtype=BF16):
    return pltpu.VMEM((rows, width), dtype)


def ring(x, axis, by):
    size = lax.axis_size(axis)
    return lax.ppermute(x, axis, [(i, (i + by) % size) for i in range(size)])


def call(body, outs, args, scratch, name, smem=0):
    def kernel(*refs):
        body(Copies(refs[-1]), *refs[:-1])

    return pl.pallas_call(
        kernel,
        out_shape=[jax.ShapeDtypeStruct(s, d) for s, d in outs],
        in_specs=[SM] * smem + [ANY] * (len(args) - smem),
        out_specs=[ANY] * len(outs),
        scratch_shapes=list(scratch) + [pltpu.SemaphoreType.DMA((32,))],
        cost_estimate=pl.CostEstimate(flops=20_000_000_000, bytes_accessed=0, transcendentals=0),
        compiler_params=pltpu.CompilerParams(vmem_limit_bytes=60 * 2**20),
        name=name,
    )(*args)


class Copies:
    def __init__(self, sems):
        self.sems, self.count = sems, 0

    def go(self, src, dst):
        copy = self.of(src, dst)
        copy.start()
        return copy

    def of(self, src, dst):
        copy = pltpu.make_async_copy(src, dst, self.sems.at[self.count])
        self.count += 1
        return copy

    def pick(self, when, src, other, dst):
        copy = self.of(src, dst)
        instead = pltpu.make_async_copy(other, dst, self.sems.at[self.count - 1])
        pl.when(when)(copy.start)
        pl.when(jnp.logical_not(when))(instead.start)
        return copy


def nt(a, b):
    return lax.dot_general(a, b, (((1,), (1,)), ((), ())), preferred_element_type=F32)


def nn(a, b):
    return lax.dot_general(a, b, (((1,), (0,)), ((), ())), preferred_element_type=F32)


def tn(a, b):
    return lax.dot_general(a, b, (((0,), (0,)), ((), ())), preferred_element_type=F32)


def inverse_length(values):
    return lax.rsqrt(jnp.sum(values * values, axis=-1, keepdims=True) + 1e-06)


def unit_kernel(
    copies, ids_ref, cap_ref, pic_ref, text_out, image_out, wrap_out, turn_out,
    cap, pic, text, image, wrap, turns,
):
    x, core = lax.axis_index("x"), lax.axis_index("c")
    come = [
        [copies.go(src.at[pl.ds(k * HALF, HALF)], dst.at[pl.ds(k * HALF, HALF)])
         for src, dst in ((cap_ref, cap), (pic_ref, pic))]
        for k in range(2)
    ]
    row = lax.broadcasted_iota(jnp.int32, (16, BLOCK), 0)
    image[pl.ds(ROWS, 16), :] = jnp.zeros((16, WIDTH), BF16)
    for n in range(3):
        count = jnp.zeros((16, BLOCK), F32)
        for owner in range(8):
            hit = [jnp.where(ids_ref[c, owner] == n, 1.0, 0.0) for c in range(2)]
            count = jnp.where(row == owner, hit[0] + hit[1], count)
        image[pl.ds(ROWS, 16), pl.ds(n * BLOCK, BLOCK)] = count.astype(BF16)
    leave = []
    for k in range(2):
        at = pl.ds(k * HALF, HALF)
        come[k][0].wait()
        v = cap[at, :].astype(F32)
        t = (v * inverse_length(v)).astype(BF16)
        text[at, :] = t
        come[k][1].wait()
        v = pic[at, :].astype(F32)
        i = (v * inverse_length(v)).astype(BF16)
        image[at, :] = i
        wrap[at, :] = jnp.where(x >= 2, t, i)
        for j in range(4):
            ahead = jnp.logical_or(x < j, jnp.logical_and(x == j, core == 0))
            turns[j, at, :] = jnp.where(ahead, t, i)
        for src, dst in ((text, text_out), (wrap, wrap_out)):
            leave.append(copies.go(src.at[at], dst.at[at]))
        for j in range(4):
            leave.append(copies.go(turns.at[j, at], turn_out.at[j, at]))
        if k == 0:
            leave.append(copies.go(image.at[at], image_out.at[at]))
        else:
            rest = pl.ds(HALF, HALF + 16)
            leave.append(copies.go(image.at[rest], image_out.at[rest]))
    for copy in leave:
        copy.wait()


def weights(scores, par_ref):
    half = par_ref[0] * 0.5
    return half + half * jnp.tanh(half * scores + par_ref[1] * 0.5)


def slot_count(counts, owner, block):
    values = counts[pl.ds(0, 16), pl.ds(block * BLOCK, BLOCK)].astype(F32)
    row = lax.broadcasted_iota(jnp.int32, (16, BLOCK), 0)
    return jnp.sum(jnp.where(row == owner, values, 0.0), axis=0, keepdims=True)


def hard_weights(text, x_scr, wt_ref, row, par_ref, near, far, owner, own):
    for j in range(3):
        w = weights(nt(text, x_scr[pl.ds(j * 256, 256), :]), par_ref)
        if own and j < 2:
            r = lax.broadcasted_iota(jnp.int32, (ROWS, 256), 0)
            q = lax.broadcasted_iota(jnp.int32, (ROWS, 256), 1) + j * 256
            w = jnp.where(r == q, w - par_ref[0], w)
        w = w.astype(BF16)
        for n in range(3):
            rows = slice(n * BLOCK, (n + 1) * BLOCK)
            for h in range(2):
                col = j * 256 + h * 128
                part = w[rows, h * 128 : (h + 1) * 128]
                if col >= ROWS or not own:
                    count = slot_count(near if col < ROWS else far, owner, n)
                    part = (part.astype(F32) * count).astype(BF16)
                wt_ref[pl.ds(row + n * BLOCK, BLOCK), pl.ds(col, 128)] = part


def owners():
    y, zl, core = lax.axis_index("y"), lax.axis_index("zl"), lax.axis_index("c")
    return [lax.rem(y + step, 4) * 2 + zl for step in (3 - 2 * core, 1 + 2 * core, 0, 2)]


def fetch_images(copies, image_ref, other_ref, x_scr, near, far):
    rows, rest = pl.ds(0, ROWS), pl.ds(ROWS, 16)
    return [
        copies.go(image_ref.at[rest], near),
        copies.go(other_ref.at[rest], far),
        copies.go(image_ref.at[rows], x_scr.at[rows]),
        copies.go(other_ref.at[rows], x_scr.at[pl.ds(ROWS, ROWS)]),
    ]


def hard_kernel(
    copies, par_ref, image_ref, other_ref, one_ref, two_ref, text_ref, after_ref,
    early_out, late_out, gt_out, wt_out, x_scr, near, far, t_scr, early, late, gt, wt,
):
    images = fetch_images(copies, image_ref, other_ref, x_scr, near, far)
    texts = [copies.go(ref, t_scr.at[k]) for k, ref in enumerate((one_ref, two_ref, text_ref))]
    owner = owners()
    for copy in images:
        copy.wait()
    leave = []
    for k in range(3):
        texts[k].wait()
        hard_weights(t_scr[k], x_scr, wt, k * ROWS, par_ref, near, far, owner[k], k == 2)
        p = nn(wt[pl.ds(k * ROWS, ROWS), :], x_scr[...])
        if k == 0:
            early[...] = p.astype(BF16)
        else:
            (late, gt)[k - 1][...] = p
        src, dst = ((early, early_out), (late, late_out), (gt, gt_out))[k]
        leave.append(copies.go(src, dst))
    leave.append(copies.go(wt, wt_out))
    for copy in leave:
        copy.wait()


def opposite_kernel(
    copies, par_ref, image_ref, other_ref, opp_ref, after_ref, return_out, wt_out,
    x_scr, near, far, text, back, wt,
):
    images = fetch_images(copies, image_ref, other_ref, x_scr, near, far)
    images.append(copies.go(opp_ref, text))
    for copy in images:
        copy.wait()
    hard_weights(text[...], x_scr, wt, 0, par_ref, near, far, owners()[3], False)
    leave = [copies.go(wt, wt_out)]
    back[...] = nn(wt[...], x_scr[...]).astype(BF16)
    leave.append(copies.go(back, return_out))
    for copy in leave:
        copy.wait()


def image_kernel(
    copies, wt3_ref, wt_ref, one_ref, two_ref, text_ref, opp_ref, far_out, near_out,
    w_scr, t_scr, far, near,
):
    come = [
        copies.go(wt3_ref, w_scr.at[pl.ds(0, 3 * ROWS)]),
        copies.go(wt_ref, w_scr.at[pl.ds(3 * ROWS, ROWS)]),
    ]
    for k, ref in enumerate((one_ref, two_ref, text_ref, opp_ref)):
        come.append(copies.go(ref, t_scr.at[pl.ds(k * ROWS, ROWS)]))
    for copy in come:
        copy.wait()
    far[...] = tn(w_scr[:, ROWS:], t_scr[...]).astype(BF16)
    leave = [copies.go(far, far_out)]
    near[...] = tn(w_scr[:, :ROWS], t_scr[...])
    leave.append(copies.go(near, near_out))
    for copy in leave:
        copy.wait()


def attend(mine, scr, w_scr, par_ref, count):
    for j in range(count * 3 // 2):
        at = pl.ds(j * 256, 256)
        w_scr[:, at] = weights(nt(mine, scr[at, :]), par_ref).astype(BF16)
    return nn(w_scr[:, : count * ROWS], scr[: count * ROWS, :])


def cycle_kernel(
    copies, par_ref, image_ref, text_ref, own, sib, aw, sa, bw, sb, gi_ref, gt_ref,
    after_ref, early_ref, gi_out, gt_out, image, text, gi, gt, t_scr, i_scr, w_scr,
):
    x, core = lax.axis_index("x"), lax.axis_index("c")
    come = []
    for low, mine_ref, mine, grad_ref, grad, scr in (
        (True, image_ref, image, gi_ref, gi, t_scr),
        (False, text_ref, text, gt_ref, gt, i_scr),
    ):
        d = x if low else 3 - x
        e = core if low else 1 - core
        at = lambda ref, i: ref.at[jnp.clip(i if low else 3 - i, 0, 3)]
        slot = lambda k: scr.at[pl.ds(k * ROWS, ROWS)]
        last = d - 2 + e
        here = [
            copies.go(mine_ref.at[pl.ds(0, ROWS)], mine),
            copies.pick(d >= 1, at(own, d - 1), aw, slot(0)),
            copies.pick(d >= 2, at(own, d - 2), bw, slot(1)),
            copies.pick(d - 1 + e >= 0, at(sib, d - 1 + e), sa, slot(2)),
        ]
        copy = copies.of(sb, slot(3))
        sem = copies.sems.at[copies.count - 1]
        pl.when(last >= 0)(pltpu.make_async_copy(at(sib, last), slot(3), sem).start)
        swapped = jnp.logical_and(d == 0, e == 1)
        pl.when(swapped)(pltpu.make_async_copy(sa, slot(3), sem).start)
        pl.when(jnp.logical_and(last < 0, jnp.logical_not(swapped)))(copy.start)
        here.append(copy)
        here.append(copies.go(grad_ref, grad))
        come.append(here)
    leave = []
    for here, mine, grad, scr, out in (
        (come[0], image, gi, t_scr, gi_out),
        (come[1], text, gt, i_scr, gt_out),
    ):
        for copy in here:
            copy.wait()
        grad[...] += attend(mine[...], scr, w_scr, par_ref, 4)
        leave.append(copies.go(grad, out))
    for copy in leave:
        copy.wait()


def add_kernel(copies, late_ref, return_ref, after_ref, out_ref, late, back, out):
    come = [copies.go(late_ref, late), copies.go(return_ref, back)]
    for copy in come:
        copy.wait()
    out[...] = (late[...] + back[...].astype(F32)).astype(BF16)
    copies.go(out, out_ref).wait()


def gate_kernel(block_ref, after_ref, out_ref):
    pass


def through_norm(raw, grads):
    values = raw.astype(F32)
    inv = inverse_length(values)
    unit = values * inv
    inner = jnp.sum(unit * grads, axis=-1, keepdims=True)
    return (grads - unit * inner) * inv


def last_kernel(
    copies, par_ref, f, f1, image_ref, text_ref, pic_ref, gi_ref, back_ref, cap_ref, gt_ref,
    early_ref, late_ref, image_out, text_out,
    scr, w_scr, mine, more, pic, gi, back, cap, gt, early, late,
):
    x = lax.axis_index("x")
    come = [
        copies.go(f, scr.at[pl.ds(0, ROWS)]),
        copies.go(f1, scr.at[pl.ds(ROWS, ROWS)]),
        copies.pick(x <= 1, image_ref.at[pl.ds(0, ROWS)], text_ref, mine),
    ]
    rest = [
        copies.go(src, dst)
        for src, dst in (
            (pic_ref, pic), (gi_ref, gi), (back_ref, back), (cap_ref, cap), (gt_ref, gt),
            (early_ref, early), (late_ref, late),
        )
    ]
    for copy in come:
        copy.wait()

    @pl.when(jnp.logical_or(x == 1, x == 2))
    def _():
        more[...] = attend(mine[...], scr, w_scr, par_ref, 2)

    for copy in rest:
        copy.wait()
    leave = []
    for k in range(3):
        at = pl.ds(k * BLOCK, BLOCK)
        g = gi[at, :] + back[at, :].astype(F32)
        g = jnp.where(x == 1, g + more[at, :], g)
        gi[at, :] = through_norm(pic[at, :], g)
        leave.append(copies.go(gi.at[at], image_out.at[at]))
        g = gt[at, :] + early[at, :].astype(F32) + late[at, :].astype(F32)
        g = jnp.where(x == 2, g + more[at, :], g)
        gt[at, :] = through_norm(cap[at, :], g)
        leave.append(copies.go(gt.at[at], text_out.at[at]))
    for copy in leave:
        copy.wait()


def gate(block, after):
    return pl.pallas_call(
        gate_kernel,
        out_shape=jax.ShapeDtypeStruct(block.shape, block.dtype),
        in_specs=[ANY, ANY],
        out_specs=ANY,
        input_output_aliases={0: 0},
        compiler_params=pltpu.CompilerParams(vmem_limit_bytes=60 * 2**20),
        name="gate",
    )(block, after)


def local(pictures, captions, sharpness, offset, tile_numbers):
    pics, caps = pictures[0, 0], captions[0, 0]
    par = jnp.stack([sharpness, offset])
    counts = [vm(16), vm(16)]
    text, image, wrap, turns = call(
        unit_kernel,
        [WHOLE, ((ROWS + 16, WIDTH), BF16), WHOLE, ((4, ROWS, WIDTH), BF16)],
        (tile_numbers[0, 0].T, caps, pics),
        [vm(ROWS), vm(ROWS), vm(ROWS), vm(ROWS + 16), vm(ROWS), pltpu.VMEM((4, ROWS, WIDTH), BF16)],
        "unit",
        1,
    )

    def along_y(block, way):
        pairs = []
        for y in range(4):
            pairs += [(y, (y + way) % 4), (4 + y, 4 + (y - way) % 4)]
        return lax.ppermute(block, ("c", "y"), pairs)

    turn = lambda x, c: x * 2 + c
    with jax.named_scope("one"):
        text_one = along_y(text, 1)
    with jax.named_scope("other"):
        other = ring(image, "zl", 1)
    with jax.named_scope("two"):
        text_two = along_y(text, -1)
    with jax.named_scope("hop"):
        hop = lax.ppermute(
            wrap,
            ("x", "c"),
            [(turn(x, 0), turn(x, 0)) for x in range(4)]
            + [(turn(a, 1), turn(b, 1)) for a, b in ((3, 0), (2, 1), (1, 2), (0, 3))],
        )
    with jax.named_scope("turns"):
        own = lax.all_to_all(turns, "x", split_axis=0, concat_axis=0, tiled=True)
    with jax.named_scope("opp"):
        text_opp = along_y(text_one, 1)
    hop = gate(hop, other)

    def over(pairs):
        sends = []
        for z in range(4):
            for a, b, c, d in pairs:
                sends.append((z * 8 + turn(a, c), (z + d) % 4 * 8 + turn(b, c)))
        return lax.ppermute(hop, GROUP, sends)

    with jax.named_scope("over_a"):
        over_a = over([(3, 0, 0, 1), (0, 3, 0, -1), (0, 0, 1, 1), (3, 3, 1, -1)])
    with jax.named_scope("over_b"):
        over_b = over([(2, 0, 0, 1), (1, 3, 0, -1), (1, 0, 1, 1), (2, 3, 1, -1)])

    part_early, part_late, grad_text, wt3 = call(
        hard_kernel,
        [WHOLE, WHOLE32, WHOLE32, ((3 * ROWS, 2 * ROWS), BF16)],
        (par, image, other, text_one, text_two, text, hop),
        [vm(2 * ROWS), *counts, pltpu.VMEM((3, ROWS, WIDTH), BF16), vm(ROWS),
         vm(ROWS, dtype=F32), vm(ROWS, dtype=F32), vm(3 * ROWS, 2 * ROWS)],
        "hard",
        1,
    )
    with jax.named_scope("early"):
        early = along_y(part_early, -1)
    part_opp, wt = call(
        opposite_kernel,
        [WHOLE, ((ROWS, 2 * ROWS), BF16)],
        (par, image, other, text_opp, part_early),
        [vm(2 * ROWS), *counts, vm(ROWS), vm(ROWS), vm(ROWS, 2 * ROWS)],
        "opposite",
        1,
    )
    with jax.named_scope("carried"):
        carried = along_y(part_opp, 1)
    own = gate(own, part_opp)
    with jax.named_scope("sib"):
        sib = ring(own, "c", 1)
    grad_far, grad_image = call(
        image_kernel,
        [WHOLE, WHOLE32],
        (wt3, wt, text_one, text_two, text, text_opp),
        [vm(4 * ROWS, 2 * ROWS), vm(4 * ROWS), vm(ROWS), vm(ROWS, dtype=F32)],
        "image_side",
    )
    with jax.named_scope("back"):
        grad_back = ring(grad_far, "zl", 1)
    part_late = call(
        add_kernel,
        [WHOLE],
        (part_late, carried, grad_far),
        [vm(ROWS, dtype=F32), vm(ROWS), vm(ROWS)],
        "add",
    )[0]
    with jax.named_scope("late"):
        late = along_y(part_late, 1)

    with jax.named_scope("over_f"):
        over_f = lax.ppermute(over_a, "x", [(0, 1), (3, 2)])
    with jax.named_scope("over_a1"):
        over_a1 = ring(over_a, "c", 1)
    with jax.named_scope("over_b1"):
        over_b1 = lax.ppermute(
            over_b, ("x", "c"), [(turn(0, 1), turn(0, 0)), (turn(3, 0), turn(3, 1))]
        )
    grad_image, grad_text = call(
        cycle_kernel,
        [WHOLE32, WHOLE32],
        (par, image, text, own, sib, over_a, over_a1, over_b, over_b1, grad_image, grad_text,
         part_late, early),
        [vm(ROWS), vm(ROWS), vm(ROWS, dtype=F32), vm(ROWS, dtype=F32), vm(4 * ROWS),
         vm(4 * ROWS), vm(ROWS, 4 * ROWS)],
        "cycle",
        1,
    )
    over_f = gate(over_f, grad_image)
    with jax.named_scope("over_f1"):
        over_f1 = lax.ppermute(
            over_f, ("x", "c"), [(turn(1, 1), turn(1, 0)), (turn(2, 0), turn(2, 1))]
        )
    image_grad, text_grad = call(
        last_kernel,
        [WHOLE32, WHOLE32],
        (par, over_f, over_f1, image, text, pics, grad_image, grad_back, caps, grad_text,
         early, late),
        [vm(2 * ROWS), vm(ROWS, 2 * ROWS), vm(ROWS), vm(ROWS, dtype=F32), vm(ROWS),
         vm(ROWS, dtype=F32), vm(ROWS), vm(ROWS), vm(ROWS, dtype=F32), vm(ROWS), vm(ROWS)],
        "last",
        1,
    )
    return (image_grad[None, None], text_grad[None, None])


def solution(mesh):
    fine = Mesh(mesh.devices.reshape(4, 4, 2, 4, 2), GROUP + BULK)
    spec = P(GROUP, BULK, None, None)
    return jax.shard_map(
        local,
        mesh=fine,
        in_specs=(spec, spec, P(), P(), spec),
        out_specs=(spec, spec),
        check_vma=False,
    )
```

```python
import jax
import jax.numpy as jnp
from jax import lax
from jax.experimental import pallas as pl
from jax.experimental.pallas import tpu as pltpu
from jax.sharding import Mesh, PartitionSpec as P

ROWS = 384
HALF = 192
BLOCK = 128
WIDTH = 1152
GROUP = ("zh", "x", "c")
BULK = ("y", "zl")
BF16 = jnp.bfloat16
F32 = jnp.float32
SM = pl.BlockSpec(memory_space=pltpu.SMEM)
ANY = pl.BlockSpec(memory_space=pltpu.HBM)
WHOLE, WHOLE32 = ((ROWS, WIDTH), BF16), ((ROWS, WIDTH), F32)


def vm(rows, width=WIDTH, dtype=BF16):
    return pltpu.VMEM((rows, width), dtype)


def ring(x, axis, by):
    size = lax.axis_size(axis)
    return lax.ppermute(x, axis, [(i, (i + by) % size) for i in range(size)])


def call(body, outs, args, scratch, name, smem=0):
    def kernel(*refs):
        body(Copies(refs[-1]), *refs[:-1])

    return pl.pallas_call(
        kernel,
        out_shape=[jax.ShapeDtypeStruct(s, d) for s, d in outs],
        in_specs=[SM] * smem + [ANY] * (len(args) - smem),
        out_specs=[ANY] * len(outs),
        scratch_shapes=list(scratch) + [pltpu.SemaphoreType.DMA((32,))],
        cost_estimate=pl.CostEstimate(flops=1 if name in ("opposite", "image_side") else 20_000_000_000, bytes_accessed=0, transcendentals=0),
        compiler_params=pltpu.CompilerParams(vmem_limit_bytes=60 * 2**20),
        name=name,
    )(*args)


class Copies:
    def __init__(self, sems):
        self.sems, self.count = sems, 0

    def go(self, src, dst):
        copy = self.of(src, dst)
        copy.start()
        return copy

    def of(self, src, dst):
        copy = pltpu.make_async_copy(src, dst, self.sems.at[self.count])
        self.count += 1
        return copy

    def pick(self, when, src, other, dst):
        copy = self.of(src, dst)
        instead = pltpu.make_async_copy(other, dst, self.sems.at[self.count - 1])
        pl.when(when)(copy.start)
        pl.when(jnp.logical_not(when))(instead.start)
        return copy


def nt(a, b):
    return lax.dot_general(a, b, (((1,), (1,)), ((), ())), preferred_element_type=F32)


def nn(a, b):
    return lax.dot_general(a, b, (((1,), (0,)), ((), ())), preferred_element_type=F32)


def tn(a, b):
    return lax.dot_general(a, b, (((0,), (0,)), ((), ())), preferred_element_type=F32)


def inverse_length(values):
    return lax.rsqrt(jnp.sum(values * values, axis=-1, keepdims=True) + 1e-06)


def unit_kernel(
    copies, ids_ref, cap_ref, pic_ref, text_out, image_out, wrap_out, turn_out,
    cap, pic, text, image, wrap, turns,
):
    x, core = lax.axis_index("x"), lax.axis_index("c")
    come = [
        [copies.go(src.at[pl.ds(k * HALF, HALF)], dst.at[pl.ds(k * HALF, HALF)])
         for src, dst in ((cap_ref, cap), (pic_ref, pic))]
        for k in range(2)
    ]
    row = lax.broadcasted_iota(jnp.int32, (16, BLOCK), 0)
    image[pl.ds(ROWS, 16), :] = jnp.zeros((16, WIDTH), BF16)
    for n in range(3):
        count = jnp.zeros((16, BLOCK), F32)
        for owner in range(8):
            hit = [jnp.where(ids_ref[c, owner] == n, 1.0, 0.0) for c in range(2)]
            count = jnp.where(row == owner, hit[0] + hit[1], count)
        image[pl.ds(ROWS, 16), pl.ds(n * BLOCK, BLOCK)] = count.astype(BF16)
    leave = []
    for k in range(2):
        at = pl.ds(k * HALF, HALF)
        come[k][0].wait()
        v = cap[at, :].astype(F32)
        t = (v * inverse_length(v)).astype(BF16)
        text[at, :] = t
        come[k][1].wait()
        v = pic[at, :].astype(F32)
        i = (v * inverse_length(v)).astype(BF16)
        image[at, :] = i
        wrap[at, :] = jnp.where(x >= 2, t, i)
        for j in range(4):
            ahead = jnp.logical_or(x < j, jnp.logical_and(x == j, core == 0))
            turns[j, at, :] = jnp.where(ahead, t, i)
        for src, dst in ((text, text_out), (wrap, wrap_out)):
            leave.append(copies.go(src.at[at], dst.at[at]))
        for j in range(4):
            leave.append(copies.go(turns.at[j, at], turn_out.at[j, at]))
        if k == 0:
            leave.append(copies.go(image.at[at], image_out.at[at]))
        else:
            rest = pl.ds(HALF, HALF + 16)
            leave.append(copies.go(image.at[rest], image_out.at[rest]))
    for copy in leave:
        copy.wait()


def weights(scores, par_ref):
    half = par_ref[0] * 0.5
    return half + half * jnp.tanh(half * scores + par_ref[1] * 0.5)


def slot_count(counts, owner, block):
    values = counts[pl.ds(0, 16), pl.ds(block * BLOCK, BLOCK)].astype(F32)
    row = lax.broadcasted_iota(jnp.int32, (16, BLOCK), 0)
    return jnp.sum(jnp.where(row == owner, values, 0.0), axis=0, keepdims=True)


def hard_weights(text, x_scr, wt_ref, row, par_ref, near, far, owner, own):
    for j in range(3):
        w = weights(nt(text, x_scr[pl.ds(j * 256, 256), :]), par_ref)
        if own and j < 2:
            r = lax.broadcasted_iota(jnp.int32, (ROWS, 256), 0)
            q = lax.broadcasted_iota(jnp.int32, (ROWS, 256), 1) + j * 256
            w = jnp.where(r == q, w - par_ref[0], w)
        w = w.astype(BF16)
        for n in range(3):
            rows = slice(n * BLOCK, (n + 1) * BLOCK)
            for h in range(2):
                col = j * 256 + h * 128
                part = w[rows, h * 128 : (h + 1) * 128]
                if col >= ROWS or not own:
                    count = slot_count(near if col < ROWS else far, owner, n)
                    part = (part.astype(F32) * count).astype(BF16)
                wt_ref[pl.ds(row + n * BLOCK, BLOCK), pl.ds(col, 128)] = part


def owners():
    y, zl, core = lax.axis_index("y"), lax.axis_index("zl"), lax.axis_index("c")
    return [lax.rem(y + step, 4) * 2 + zl for step in (3 - 2 * core, 1 + 2 * core, 0, 2)]


def fetch_images(copies, image_ref, other_ref, x_scr, near, far):
    rows, rest = pl.ds(0, ROWS), pl.ds(ROWS, 16)
    return [
        copies.go(image_ref.at[rest], near),
        copies.go(other_ref.at[rest], far),
        copies.go(image_ref.at[rows], x_scr.at[rows]),
        copies.go(other_ref.at[rows], x_scr.at[pl.ds(ROWS, ROWS)]),
    ]


def hard_kernel(
    copies, par_ref, image_ref, other_ref, one_ref, two_ref, text_ref, after_ref,
    early_out, late_out, gt_out, wt_out, x_scr, near, far, t_scr, early, late, gt, wt,
):
    images = fetch_images(copies, image_ref, other_ref, x_scr, near, far)
    texts = [copies.go(ref, t_scr.at[k]) for k, ref in enumerate((one_ref, two_ref, text_ref))]
    owner = owners()
    for copy in images:
        copy.wait()
    leave = []
    for k in range(3):
        texts[k].wait()
        hard_weights(t_scr[k], x_scr, wt, k * ROWS, par_ref, near, far, owner[k], k == 2)
        p = nn(wt[pl.ds(k * ROWS, ROWS), :], x_scr[...])
        if k == 0:
            early[...] = p.astype(BF16)
        else:
            (late, gt)[k - 1][...] = p
        src, dst = ((early, early_out), (late, late_out), (gt, gt_out))[k]
        leave.append(copies.go(src, dst))
    leave.append(copies.go(wt, wt_out))
    for copy in leave:
        copy.wait()


def opposite_kernel(
    copies, par_ref, image_ref, other_ref, opp_ref, after_ref, return_out, wt_out,
    x_scr, near, far, text, back, wt,
):
    images = fetch_images(copies, image_ref, other_ref, x_scr, near, far)
    images.append(copies.go(opp_ref, text))
    for copy in images:
        copy.wait()
    hard_weights(text[...], x_scr, wt, 0, par_ref, near, far, owners()[3], False)
    leave = [copies.go(wt, wt_out)]
    back[...] = nn(wt[...], x_scr[...]).astype(BF16)
    leave.append(copies.go(back, return_out))
    for copy in leave:
        copy.wait()


def image_kernel(
    copies, wt3_ref, wt_ref, one_ref, two_ref, text_ref, opp_ref, after_ref, then_ref, again_ref,
    far_out, near_out,
    w_scr, t_scr, far, near,
):
    come = [
        copies.go(wt3_ref, w_scr.at[pl.ds(0, 3 * ROWS)]),
        copies.go(wt_ref, w_scr.at[pl.ds(3 * ROWS, ROWS)]),
    ]
    for k, ref in enumerate((one_ref, two_ref, text_ref, opp_ref)):
        come.append(copies.go(ref, t_scr.at[pl.ds(k * ROWS, ROWS)]))
    for copy in come:
        copy.wait()
    far[...] = tn(w_scr[:, ROWS:], t_scr[...]).astype(BF16)
    leave = [copies.go(far, far_out)]
    near[...] = tn(w_scr[:, :ROWS], t_scr[...])
    leave.append(copies.go(near, near_out))
    for copy in leave:
        copy.wait()


def attend(mine, scr, w_scr, par_ref, count):
    for j in range(count * 3 // 2):
        at = pl.ds(j * 256, 256)
        w_scr[:, at] = weights(nt(mine, scr[at, :]), par_ref).astype(BF16)
    return nn(w_scr[:, : count * ROWS], scr[: count * ROWS, :])


def cycle_kernel(
    copies, par_ref, image_ref, text_ref, own, sib, aw, sa, bw, sb, gi_ref, gt_ref,
    after_ref, early_ref, gi_out, gt_out, image, text, gi, gt, t_scr, i_scr, w_scr,
):
    x, core = lax.axis_index("x"), lax.axis_index("c")
    come = []
    for low, mine_ref, mine, grad_ref, grad, scr in (
        (True, image_ref, image, gi_ref, gi, t_scr),
        (False, text_ref, text, gt_ref, gt, i_scr),
    ):
        d = x if low else 3 - x
        e = core if low else 1 - core
        at = lambda ref, i: ref.at[jnp.clip(i if low else 3 - i, 0, 3)]
        slot = lambda k: scr.at[pl.ds(k * ROWS, ROWS)]
        last = d - 2 + e
        here = [
            copies.go(mine_ref.at[pl.ds(0, ROWS)], mine),
            copies.pick(d >= 1, at(own, d - 1), aw, slot(0)),
            copies.pick(d >= 2, at(own, d - 2), bw, slot(1)),
            copies.pick(d - 1 + e >= 0, at(sib, d - 1 + e), sa, slot(2)),
        ]
        copy = copies.of(sb, slot(3))
        sem = copies.sems.at[copies.count - 1]
        pl.when(last >= 0)(pltpu.make_async_copy(at(sib, last), slot(3), sem).start)
        swapped = jnp.logical_and(d == 0, e == 1)
        pl.when(swapped)(pltpu.make_async_copy(sa, slot(3), sem).start)
        pl.when(jnp.logical_and(last < 0, jnp.logical_not(swapped)))(copy.start)
        here.append(copy)
        here.append(copies.go(grad_ref, grad))
        come.append(here)
    leave = []
    for here, mine, grad, scr, out in (
        (come[0], image, gi, t_scr, gi_out),
        (come[1], text, gt, i_scr, gt_out),
    ):
        for copy in here:
            copy.wait()
        grad[...] += attend(mine[...], scr, w_scr, par_ref, 4)
        leave.append(copies.go(grad, out))
    for copy in leave:
        copy.wait()


def add_kernel(copies, late_ref, return_ref, after_ref, then_ref, out_ref, late, back, out):
    come = [copies.go(late_ref, late), copies.go(return_ref, back)]
    for copy in come:
        copy.wait()
    out[...] = (late[...] + back[...].astype(F32)).astype(BF16)
    copies.go(out, out_ref).wait()


def gate_kernel(block_ref, after_ref, out_ref):
    pass


def through_norm(raw, grads):
    values = raw.astype(F32)
    inv = inverse_length(values)
    unit = values * inv
    inner = jnp.sum(unit * grads, axis=-1, keepdims=True)
    return (grads - unit * inner) * inv


def last_kernel(
    copies, par_ref, f, f1, image_ref, text_ref, pic_ref, gi_ref, back_ref, cap_ref, gt_ref,
    early_ref, late_ref, image_out, text_out,
    scr, w_scr, mine, more, pic, gi, back, cap, gt, early, late,
):
    x = lax.axis_index("x")
    come = [
        copies.go(f, scr.at[pl.ds(0, ROWS)]),
        copies.go(f1, scr.at[pl.ds(ROWS, ROWS)]),
        copies.pick(x <= 1, image_ref.at[pl.ds(0, ROWS)], text_ref, mine),
    ]
    rest = [
        copies.go(src, dst)
        for src, dst in (
            (pic_ref, pic), (gi_ref, gi), (back_ref, back), (cap_ref, cap), (gt_ref, gt),
            (early_ref, early), (late_ref, late),
        )
    ]
    for copy in come:
        copy.wait()

    @pl.when(jnp.logical_or(x == 1, x == 2))
    def _():
        more[...] = attend(mine[...], scr, w_scr, par_ref, 2)

    for copy in rest:
        copy.wait()
    leave = []
    for k in range(3):
        at = pl.ds(k * BLOCK, BLOCK)
        g = gi[at, :] + back[at, :].astype(F32)
        g = jnp.where(x == 1, g + more[at, :], g)
        gi[at, :] = through_norm(pic[at, :], g)
        leave.append(copies.go(gi.at[at], image_out.at[at]))
        g = gt[at, :] + early[at, :].astype(F32) + late[at, :].astype(F32)
        g = jnp.where(x == 2, g + more[at, :], g)
        gt[at, :] = through_norm(cap[at, :], g)
        leave.append(copies.go(gt.at[at], text_out.at[at]))
    for copy in leave:
        copy.wait()


def gate(block, after):
    return pl.pallas_call(
        gate_kernel,
        out_shape=jax.ShapeDtypeStruct(block.shape, block.dtype),
        in_specs=[ANY, ANY],
        out_specs=ANY,
        input_output_aliases={0: 0},
        compiler_params=pltpu.CompilerParams(vmem_limit_bytes=60 * 2**20),
        name="gate",
    )(block, after)


def local(pictures, captions, sharpness, offset, tile_numbers):
    pics, caps = pictures[0, 0], captions[0, 0]
    par = jnp.stack([sharpness, offset])
    counts = [vm(16), vm(16)]
    text, image, wrap, turns = call(
        unit_kernel,
        [WHOLE, ((ROWS + 16, WIDTH), BF16), WHOLE, ((4, ROWS, WIDTH), BF16)],
        (tile_numbers[0, 0].T, caps, pics),
        [vm(ROWS), vm(ROWS), vm(ROWS), vm(ROWS + 16), vm(ROWS), pltpu.VMEM((4, ROWS, WIDTH), BF16)],
        "unit",
        1,
    )

    def along_y(block, way):
        pairs = []
        for y in range(4):
            pairs += [(y, (y + way) % 4), (4 + y, 4 + (y - way) % 4)]
        return lax.ppermute(block, ("c", "y"), pairs)

    turn = lambda x, c: x * 2 + c
    with jax.named_scope("one"):
        text_one = along_y(text, 1)
    with jax.named_scope("other"):
        other = ring(image, "zl", 1)
    with jax.named_scope("two"):
        text_two = along_y(text, -1)
    with jax.named_scope("hop"):
        hop = lax.ppermute(
            wrap,
            ("x", "c"),
            [(turn(x, 0), turn(x, 0)) for x in range(4)]
            + [(turn(a, 1), turn(b, 1)) for a, b in ((3, 0), (2, 1), (1, 2), (0, 3))],
        )
    with jax.named_scope("turns"):
        own = lax.all_to_all(turns, "x", split_axis=0, concat_axis=0, tiled=True)
    with jax.named_scope("opp"):
        text_opp = along_y(text_one, 1)
    hop = gate(hop, other)

    def over(pairs):
        sends = []
        for z in range(4):
            for a, b, c, d in pairs:
                sends.append((z * 8 + turn(a, c), (z + d) % 4 * 8 + turn(b, c)))
        return lax.ppermute(hop, GROUP, sends)

    with jax.named_scope("over_a"):
        over_a = over([(3, 0, 0, 1), (0, 3, 0, -1), (0, 0, 1, 1), (3, 3, 1, -1)])
    with jax.named_scope("over_b"):
        over_b = over([(2, 0, 0, 1), (1, 3, 0, -1), (1, 0, 1, 1), (2, 3, 1, -1)])

    part_early, part_late, grad_text, wt3 = call(
        hard_kernel,
        [WHOLE, WHOLE32, WHOLE32, ((3 * ROWS, 2 * ROWS), BF16)],
        (par, image, other, text_one, text_two, text, hop),
        [vm(2 * ROWS), *counts, pltpu.VMEM((3, ROWS, WIDTH), BF16), vm(ROWS),
         vm(ROWS, dtype=F32), vm(ROWS, dtype=F32), vm(3 * ROWS, 2 * ROWS)],
        "hard",
        1,
    )
    with jax.named_scope("early"):
        early = along_y(part_early, -1)
    part_opp, wt = call(
        opposite_kernel,
        [WHOLE, ((ROWS, 2 * ROWS), BF16)],
        (par, image, other, text_opp, part_early),
        [vm(2 * ROWS), *counts, vm(ROWS), vm(ROWS), vm(ROWS, 2 * ROWS)],
        "opposite",
        1,
    )
    with jax.named_scope("carried"):
        carried = along_y(part_opp, 1)
    grad_far, grad_image = call(
        image_kernel,
        [WHOLE, WHOLE32],
        (wt3, wt, text_one, text_two, text, text_opp, over_a, over_b, carried),
        [vm(4 * ROWS, 2 * ROWS), vm(4 * ROWS), vm(ROWS), vm(ROWS, dtype=F32)],
        "image_side",
    )
    with jax.named_scope("back"):
        grad_back = ring(grad_far, "zl", 1)
    own = gate(own, grad_far)
    with jax.named_scope("sib"):
        sib = ring(own, "c", 1)
    part_late = call(
        add_kernel,
        [WHOLE],
        (part_late, carried, grad_far, early),
        [vm(ROWS, dtype=F32), vm(ROWS), vm(ROWS)],
        "add",
    )[0]
    with jax.named_scope("late"):
        late = along_y(part_late, 1)

    with jax.named_scope("over_f"):
        over_f = lax.ppermute(over_a, "x", [(0, 1), (3, 2)])
    with jax.named_scope("over_a1"):
        over_a1 = ring(over_a, "c", 1)
    with jax.named_scope("over_b1"):
        over_b1 = lax.ppermute(
            over_b, ("x", "c"), [(turn(0, 1), turn(0, 0)), (turn(3, 0), turn(3, 1))]
        )
    grad_image, grad_text = call(
        cycle_kernel,
        [WHOLE32, WHOLE32],
        (par, image, text, own, sib, over_a, over_a1, over_b, over_b1, grad_image, grad_text,
         part_late, early),
        [vm(ROWS), vm(ROWS), vm(ROWS, dtype=F32), vm(ROWS, dtype=F32), vm(4 * ROWS),
         vm(4 * ROWS), vm(ROWS, 4 * ROWS)],
        "cycle",
        1,
    )
    over_f = gate(over_f, grad_image)
    with jax.named_scope("over_f1"):
        over_f1 = lax.ppermute(
            over_f, ("x", "c"), [(turn(1, 1), turn(1, 0)), (turn(2, 0), turn(2, 1))]
        )
    image_grad, text_grad = call(
        last_kernel,
        [WHOLE32, WHOLE32],
        (par, over_f, over_f1, image, text, pics, grad_image, grad_back, caps, grad_text,
         early, late),
        [vm(2 * ROWS), vm(ROWS, 2 * ROWS), vm(ROWS), vm(ROWS, dtype=F32), vm(ROWS),
         vm(ROWS, dtype=F32), vm(ROWS), vm(ROWS), vm(ROWS, dtype=F32), vm(ROWS), vm(ROWS)],
        "last",
        1,
    )
    return (image_grad[None, None], text_grad[None, None])


def solution(mesh):
    fine = Mesh(mesh.devices.reshape(4, 4, 2, 4, 2), GROUP + BULK)
    spec = P(GROUP, BULK, None, None)
    return jax.shard_map(
        local,
        mesh=fine,
        in_specs=(spec, spec, P(), P(), spec),
        out_specs=(spec, spec),
        check_vma=False,
    )
```
